512 devices in a mesh: wide: 64 (over z, x, core), narrow: 8 (over y).
Axes of the slice: x: 4, y: 8, z: 8, core: 2. Of those that a mesh axis runs over, the one named last changes fastest.
Arguments:
- inputs: bfloat16 [5, 192, 8192], P(None, 'wide', 'narrow'), may hold values from -30 to 30
- pre_gain: float32 [8192], P('narrow'), may hold values from 0.1 to 1.9
- w_z: bfloat16 [8192, 16384], P('narrow', 'wide'), may hold values from -0.0625 to 0.0625
- w_x: bfloat16 [8192, 16384], P('narrow', 'wide'), may hold values from -0.0625 to 0.0625
- w_bc: bfloat16 [8192, 4096], P('narrow', 'wide'), may hold values from -0.0625 to 0.0625
- w_dt: bfloat16 [8192, 256], P('narrow', 'wide'), may hold values from -0.0625 to 0.0625
- conv_x_w: float32 [4, 16384], P(None, 'wide'), may hold values from -1 to 1
- conv_bc_w: float32 [4, 4096], P(None, 'wide'), may hold values from -1 to 1
- conv_x_state: bfloat16 [192, 3, 16384], P('narrow', None, 'wide'), may hold values from -5 to 5
- conv_bc_state: bfloat16 [192, 3, 4096], P('narrow', None, 'wide'), may hold values from -5 to 5
- a_log: float32 [256], P('wide'), may hold values from -0.7 to 2
- dt_bias: float32 [256], P('wide'), may hold values from -3 to 0
- skip_d: float32 [256], P('wide'), may hold values from 0.5 to 1.5
- ssm_state: bfloat16 [192, 256, 64, 256], P('narrow', 'wide'), may hold values from -2 to 2
- norm_gain: float32 [16384], P('wide'), may hold values from 0.1 to 1.9
- w_out: bfloat16 [16384, 8192], P('wide', 'narrow'), may hold values from -0.046875 to 0.046875
Outputs:
- mixed: bfloat16 [5, 192, 8192], P(None, 'wide', 'narrow')
The draws below stay inside these ranges and needn't reach their ends.
All inputs are finite; a program needn't handle non-finite values.
Results may differ from the reference program's by a relative error of at most 0.018.
Values may be sent and summed in bfloat16 or wider, within the bound.
No kernel may reach another device: no remote copies, remote signals or barrier semaphores. Data moves between devices by JAX's collectives and lax.ppermute only.
A program may use at most 64 MiB of HBM per device.

```python
import math
import jax
import jax.numpy as jnp
from jax import lax

D = 8192
HEADS = 256
HDIM = 64
NSTATE = 256
GROUPS = 8
CONVK = 4
STEPS = 5
ROWS = 192
DI = 16384
BCW = 4096
N_NARROW = 8


def draw_inputs(key, part):
    key = jax.random.fold_in(key, 11)
    key_base, key_col, key_row = jax.random.split(key, 3)
    column = jnp.arange(D, dtype=jnp.float32) / D
    col_scale = jnp.exp(math.log(3.0) * (column - 0.5) + jax.random.uniform(key_col, (D,), jnp.float32, -0.35, 0.35))
    base = jnp.clip(jax.random.normal(key_base, (STEPS, ROWS, D), jnp.float32), -4.0, 4.0)
    row_scale = jnp.exp(jax.random.uniform(key_row, (STEPS, ROWS, 1), jnp.float32, math.log(0.3), math.log(3.0)))
    return jnp.clip(base * row_scale * col_scale, -30.0, 30.0).astype(jnp.bfloat16)


def level_of(stream_key, shape, cuts, least, largest):
    level, own = 1.0, jax.random.fold_in(stream_key, 6)
    for axis_at, blocks in cuts:
        heights = jnp.exp(jax.random.uniform(jax.random.fold_in(own, axis_at), (blocks,), jnp.float32, least / len(cuts), largest / len(cuts)))
        level = level * jnp.repeat(heights, shape[axis_at] // blocks).reshape([-1 if axis == axis_at else 1 for axis in range(len(shape))])
    return level


def noise(key, shape, scale, most, pieces=(), held_as=jnp.bfloat16):
    gain = level_of(key, shape, pieces, -0.22, 0.18) if pieces else 1.0
    entries = jax.random.normal(key, shape, jnp.float32) * scale * gain
    return jnp.minimum(jnp.maximum(entries, -most), most).astype(held_as)


def setup_inputs(seed: int = 0) -> dict:
    arg_keys = jax.random.split(jax.random.key(seed), 17)
    return {
        "inputs": draw_inputs(jax.random.fold_in(arg_keys[16], 71), 0),
        "pre_gain": jnp.clip(1.0 + 0.18 * jax.random.normal(arg_keys[1], (D,), jnp.float32), 0.1, 1.9),
        "w_z": noise(arg_keys[2], (D, DI), D ** -0.5, 0.0625, ((0, 8), (1, 64))),
        "w_x": noise(arg_keys[3], (D, DI), D ** -0.5, 0.0625, ((0, 8), (1, 64))),
        "w_bc": noise(arg_keys[4], (D, BCW), D ** -0.5, 0.0625, ((0, 8), (1, 64))),
        "w_dt": noise(arg_keys[5], (D, HEADS), D ** -0.5, 0.0625, ((0, 8), (1, 64))),
        "conv_x_w": jnp.clip(jax.random.uniform(arg_keys[6], (CONVK, DI), jnp.float32, -1.0, 1.0) * level_of(arg_keys[6], (CONVK, DI), ((1, 64),), -0.4, 0.0), -1.0, 1.0),
        "conv_bc_w": jnp.clip(jax.random.uniform(arg_keys[7], (CONVK, BCW), jnp.float32, -1.0, 1.0) * level_of(arg_keys[7], (CONVK, BCW), ((1, 64),), -0.4, 0.0), -1.0, 1.0),
        "conv_x_state": noise(arg_keys[8], (ROWS, CONVK - 1, DI), 1.0, 5.0, ((0, 8), (2, 64))),
        "conv_bc_state": noise(arg_keys[9], (ROWS, CONVK - 1, BCW), 1.0, 5.0, ((0, 8), (2, 64))),
        "a_log": jnp.clip(-0.7 + 2.7 * jax.random.uniform(arg_keys[10], (HEADS,), jnp.float32) ** level_of(arg_keys[10], (HEADS,), ((0, 64),), -0.2, 0.2), -0.7, 2.0),
        "dt_bias": jnp.clip(-3.0 + 3.0 * jax.random.uniform(arg_keys[11], (HEADS,), jnp.float32) ** level_of(arg_keys[11], (HEADS,), ((0, 64),), -0.2, 0.2), -3.0, 0.0),
        "skip_d": jnp.clip(0.5 + 1.0 * jax.random.uniform(arg_keys[12], (HEADS,), jnp.float32) ** level_of(arg_keys[12], (HEADS,), ((0, 64),), -0.2, 0.2), 0.5, 1.5),
        "ssm_state": noise(arg_keys[13], (ROWS, HEADS, HDIM, NSTATE), 0.3, 2.0, ((0, 8), (1, 64))),
        "norm_gain": jnp.clip(1.0 + 0.18 * jax.random.normal(arg_keys[14], (DI,), jnp.float32), 0.1, 1.9),
        "w_out": noise(arg_keys[15], (DI, D), DI ** -0.5, 0.046875, ((0, 64), (1, 8))),
    }


EPS = 1e-05

def project(normed_flat, weight):
    width = D // N_NARROW
    total = jnp.zeros((normed_flat.shape[0], weight.shape[1]), jnp.float32)
    for block in range(N_NARROW):
        part = jnp.dot(normed_flat[:, block * width:(block + 1) * width], weight[block * width:(block + 1) * width], preferred_element_type=jnp.float32)
        total = total + lax.optimization_barrier(part.astype(jnp.bfloat16)).astype(jnp.float32)
    return total.astype(jnp.bfloat16)

def convolve(history, current, taps):
    sequence = jnp.concatenate([jnp.moveaxis(history, 1, 0), current], axis=0)
    results = []
    for step in range(STEPS):
        acc = taps[0] * sequence[step].astype(jnp.float32)
        for k in range(1, CONVK):
            acc = acc + taps[k] * sequence[step + k].astype(jnp.float32)
        results.append(jax.nn.silu(acc))
    return jnp.stack(results, 0)

def reference(inputs, pre_gain, w_z, w_x, w_bc, w_dt, conv_x_w, conv_bc_w, conv_x_state, conv_bc_state, a_log, dt_bias, skip_d, ssm_state, norm_gain, w_out):
    rows = inputs.shape[1]
    tokens = inputs.astype(jnp.float32)
    square_mean = lax.optimization_barrier(jnp.mean(tokens * tokens, axis=-1, keepdims=True))
    normed = (tokens * lax.rsqrt(square_mean + EPS) * pre_gain).astype(jnp.bfloat16)
    flat = normed.reshape(STEPS * rows, D)
    gate_raw = project(flat, w_z).reshape(STEPS, rows, DI)
    head_raw = project(flat, w_x).reshape(STEPS, rows, DI)
    state_raw = project(flat, w_bc).reshape(STEPS, rows, BCW)
    step_raw = project(flat, w_dt).reshape(STEPS, rows, HEADS)
    head_conv = convolve(conv_x_state, head_raw, conv_x_w)
    state_conv = convolve(conv_bc_state, state_raw, conv_bc_w).astype(jnp.bfloat16)
    step_size = jax.nn.softplus(step_raw.astype(jnp.float32) + dt_bias)
    decay = jnp.exp(-step_size * jnp.exp(a_log))
    grouped = state_conv.reshape(STEPS, rows, GROUPS, 2, NSTATE)
    b_all = grouped[:, :, :, 0, :]
    c_all = grouped[:, :, :, 1, :]
    head_in = head_conv.reshape(STEPS, rows, HEADS, HDIM)

    def one_head(head):
        group = head // (HEADS // GROUPS)
        state = lax.dynamic_index_in_dim(ssm_state, head, 1, keepdims=False).astype(jnp.float32)
        inner = lax.dynamic_index_in_dim(head_in, head, 2, keepdims=False)
        sizes = lax.dynamic_index_in_dim(step_size, head, 2, keepdims=False)
        rates = lax.dynamic_index_in_dim(decay, head, 2, keepdims=False)
        b_head = lax.dynamic_index_in_dim(b_all, group, 2, keepdims=False).astype(jnp.float32)
        c_head = lax.dynamic_index_in_dim(c_all, group, 2, keepdims=False).astype(jnp.float32)
        outputs = []
        for step in range(STEPS):
            state = rates[step][:, None, None] * state + (sizes[step][:, None] * inner[step])[:, :, None] * b_head[step][:, None, :]
            outputs.append(lax.optimization_barrier(jnp.sum(state * c_head[step][:, None, :], axis=-1)))
            state = lax.optimization_barrier(state.astype(jnp.bfloat16)).astype(jnp.float32)
        return jnp.stack(outputs, 0)
    head_out = lax.map(one_head, jnp.arange(HEADS))
    head_out = jnp.moveaxis(head_out, 0, 2) + skip_d[None, None, :, None] * head_in
    gated = head_out.reshape(STEPS, rows, DI) * jax.nn.silu(gate_raw.astype(jnp.float32))
    parts = gated.reshape(STEPS, rows, GROUPS, DI // GROUPS)
    group_mean = lax.optimization_barrier(jnp.mean(parts * parts, axis=-1, keepdims=True))
    ynorm = ((parts * lax.rsqrt(group_mean + EPS)).reshape(STEPS, rows, DI) * norm_gain).astype(jnp.bfloat16)
    projected = jnp.dot(ynorm.reshape(STEPS * rows, DI), w_out, preferred_element_type=jnp.float32).reshape(STEPS, rows, D)
    return (tokens + projected).astype(jnp.bfloat16)
```

```python
import jax
import jax.numpy as jnp
from jax import lax
from jax.experimental import pallas as pl
from jax.experimental.pallas import tpu as pltpu
from jax.sharding import Mesh
from jax.sharding import PartitionSpec as P

D = 8192
GROUPS = 8
DI = 16384
STEPS = 5
CONVK = 4
EPS = 1e-05

NZ, NX, NC, NY = 8, 4, 2, 8
OWN = 3
SLOT = 16
HALF = NX * SLOT
BLOCK = 2 * HALF
RB = 24
BF = jnp.bfloat16
F32 = jnp.float32
WIDE = ("z", "x", "core")


def swap_core(v):
    return lax.ppermute(v, "core", [(0, 1), (1, 0)])


def to_all(v, axes, count):
    return lax.all_to_all(
        jnp.broadcast_to(v[None], (count,) + v.shape), axes, split_axis=0, concat_axis=0, tiled=True
    )


def call(kernel, out_shape, in_specs, vmem=48, **kw):
    return pl.pallas_call(
        kernel,
        out_shape=out_shape,
        in_specs=in_specs,
        compiler_params=pltpu.CompilerParams(vmem_limit_bytes=vmem * 2**20),
        **kw,
    )


VM = pl.BlockSpec(memory_space=pltpu.VMEM)
SM = pl.BlockSpec(memory_space=pltpu.SMEM)
ANY = pl.BlockSpec(memory_space=pl.ANY)


def project_kernel(g_ref, gain_ref, wz_ref, wx_ref, ws_ref, *rest):
    pz_ref, px_ref = rest[-2:]
    raw = g_ref[...].reshape(NZ * HALF, -1).astype(F32)
    ss = jnp.sum(raw * raw, axis=1, keepdims=True)
    lhs = (raw * gain_ref[...]).astype(BF)
    dot = lambda w: jnp.dot(lhs, w[...], preferred_element_type=F32)
    pz_ref[...] = dot(wz_ref).astype(pz_ref.dtype).reshape(NZ, HALF, -1)
    px_ref[:, :, :256] = dot(wx_ref).astype(BF).reshape(NZ, HALF, -1)
    small = dot(ws_ref)
    hi = ss.astype(BF).astype(F32)
    lo = ss - hi
    lane = lax.broadcasted_iota(jnp.int32, small.shape, 1)
    small = jnp.where(lane == 68, hi, jnp.where(lane == 69, lo, small))
    px_ref[:, :, 256:] = small.astype(BF).reshape(NZ, HALF, -1)


def project(g, gain, wz, wx, ws, which, held=()):
    shapes = (
        jax.ShapeDtypeStruct((NY, BLOCK, 256), BF),
        jax.ShapeDtypeStruct((NY, BLOCK, 384), BF),
    )
    specs = [
        pl.BlockSpec((NY, HALF, s.shape[2]), lambda i, w=which: (0, w, 0)) for s in shapes
    ]
    whole = lambda a: pl.BlockSpec(a.shape, lambda i, n=a.ndim: (0,) * n)
    args = (g, gain, wz, wx, ws)
    return pl.pallas_call(
        project_kernel,
        grid=(1,),
        out_shape=shapes,
        in_specs=[whole(a) for a in args] + [ANY] * len(held),
        out_specs=specs,
        input_output_aliases={len(args) + i: i for i in range(len(held))},
        compiler_params=pltpu.CompilerParams(vmem_limit_bytes=48 * 2**20),
    )(*args, *held)


def slot_of(m, core):
    half, x, j = m // HALF, m % HALF // SLOT, m % SLOT
    cc = jnp.where(half == 0, core, 1 - core)
    step = (j * 11) // 32
    q = x * 2 + cc
    return step * RB + q * OWN + (j - step * OWN), j, q


def step_from_slot(core):
    i = lax.broadcasted_iota(jnp.int32, (STEPS * RB, BLOCK), 0)
    at, j, _ = slot_of(lax.broadcasted_iota(jnp.int32, (STEPS * RB, BLOCK), 1), core)
    return jnp.where((at == i) & (j < SLOT - 1), 1.0, 0.0).astype(BF)


def slot_from_step(core):
    shape = (BLOCK, STEPS * RB)
    at, j, q = slot_of(lax.broadcasted_iota(jnp.int32, shape, 0), core)
    i = lax.broadcasted_iota(jnp.int32, shape, 1)
    row = i % RB
    last = j == SLOT - 1
    order = jnp.where((at == i) & ~last, 1.0, 0.0).astype(BF)
    collect = jnp.where((row // OWN == q) & last, 1.0, 0.0).astype(BF)
    return order, collect


def conv(hist_ref, current, taps_ref):
    seq = [hist_ref[k].astype(F32) for k in range(CONVK - 1)]
    seq += [current[t * RB : (t + 1) * RB] for t in range(STEPS)]
    out = []
    for t in range(STEPS):
        acc = taps_ref[0:1] * seq[t]
        for k in range(1, CONVK):
            acc = acc + taps_ref[k : k + 1] * seq[t + k]
        out.append(acc * jax.nn.sigmoid(acc))
    return out


def shared_kernel(core_ref, p_ref, hist_ref, taps_ref, cur_ref, rstd_ref, bcc_ref):
    total = p_ref[0].astype(F32)
    for n in range(1, NY):
        total = total + p_ref[n].astype(F32)
    ss = total[:, 256 + 68 : 256 + 69] + total[:, 256 + 69 : 256 + 70]
    rstd = lax.rsqrt(ss / D + EPS)
    raw = (total * rstd).astype(BF)
    cur = jnp.dot(step_from_slot(core_ref[0]), raw, preferred_element_type=F32)
    cur_ref[...] = cur.astype(BF)
    rstd_ref[...] = jnp.broadcast_to(rstd, rstd_ref.shape)
    for t, v in enumerate(conv(hist_ref, cur[:, 256:320], taps_ref)):
        bcc_ref[t * RB : (t + 1) * RB, :] = v.astype(BF)


def per_head(ref):
    head = lax.broadcasted_iota(jnp.int32, (1, 256), 1) // 64
    out = jnp.full((1, 256), ref[0], F32)
    for h in range(1, 4):
        out = jnp.where(head == h, ref[h], out)
    return out


def state_kernel(
    core_ref, a_log_ref, bias_ref, skip_ref, bc_ref, cur_ref, z_ref, rstd_ref, hist_ref, taps_ref,
    gain_ref, s_ref, u_ref, c_rows, y_rows,
):
    core = core_ref[0]
    at = lambda v, t: v[t * RB : (t + 1) * RB]
    b_all = jnp.concatenate([bc_ref[i] for i in range(4)], axis=1)
    c_all = jnp.concatenate([bc_ref[i] for i in range(4, 8)], axis=1)
    b_vec, c_vec = b_all.astype(F32), c_all.astype(F32)

    c_rows[...] = jnp.zeros_like(c_rows)
    for t in range(STEPS):
        for h in range(2):
            c_rows[h, pl.ds(t, RB, stride=8), :] = at(c_vec, t)[:, h * 128 : h * 128 + 128]
    for r in range(RB):
        c_row = jnp.concatenate([c_rows[h, r * 8 : r * 8 + 8, :] for h in range(2)], axis=1)
        y_row = lax.dot_general(
            c_row.astype(BF), s_ref[r], (((1,), (1,)), ((), ())), preferred_element_type=F32
        )
        for h in range(2):
            y_rows[h, r * 8 : r * 8 + 8, :] = y_row[:, h * 128 : h * 128 + 128]

    cur = cur_ref[...]
    lane = lax.broadcasted_iota(jnp.int32, (128, 256), 0)
    head = lax.broadcasted_iota(jnp.int32, (128, 256), 1) // 64
    spread = jnp.where(lane == head + 64, 1.0, 0.0).astype(BF)
    dt_raw = jnp.dot(cur[:, 256:], spread, preferred_element_type=F32)
    pre = dt_raw + per_head(bias_ref)
    dt = jnp.maximum(pre, 0.0) + jnp.log1p(jnp.exp(-jnp.abs(pre)))
    decay = jnp.exp(-dt * jnp.exp(per_head(a_log_ref)))
    skip = per_head(skip_ref)

    gate_raw = (z_ref[...].astype(F32) * rstd_ref[:, :1]).astype(BF)
    gate = jnp.dot(step_from_slot(core), gate_raw, preferred_element_type=F32)
    gate = gate * jax.nn.sigmoid(gate)

    inner = conv(hist_ref, cur[:, :256].astype(F32), taps_ref)
    carried, terms, gated = None, [], []
    for t in range(STEPS):
        d = at(decay, t)
        carried = d if carried is None else carried * d
        terms = [term * d for term in terms] + [at(dt, t) * inner[t]]
        held = [y_rows[h, pl.ds(t, RB, stride=8), :] for h in range(2)]
        y = carried * jnp.concatenate(held, axis=1) + skip * inner[t]
        for s in range(t + 1):
            y = y + jnp.sum(at(c_vec, t) * at(b_vec, s), axis=1, keepdims=True) * terms[s]
        gated.append(y * at(gate, t))
    gated = jnp.concatenate(gated, axis=0)
    ss = jnp.sum(gated * gated, axis=1, keepdims=True)
    hi = ss.astype(BF).astype(F32)
    lo = ss - hi
    row = lax.broadcasted_iota(jnp.int32, gated.shape, 0)
    lane = lax.broadcasted_iota(jnp.int32, gated.shape, 1)
    slot = row // RB * OWN + row % RB % OWN
    sums = jnp.where(lane == slot, hi, jnp.where(lane == slot + SLOT, lo, 0.0)).astype(BF)
    order, collect = slot_from_step(core)
    u = jnp.dot(order, (gated * gain_ref[...]).astype(BF), preferred_element_type=F32)
    u_ref[...] = (u + jnp.dot(collect, sums, preferred_element_type=F32)).astype(BF)


def out_kernel(u_ref, w_ref, w_other_ref, o_ref):
    mine = u_ref[:, 0].reshape(NY * HALF, 256)
    other = u_ref[:, 1].reshape(NY * HALF, 256)
    ss = mine[:, :128].astype(F32) + other[:, :128].astype(F32)
    lane = lax.broadcasted_iota(jnp.int32, ss.shape, 1)
    ss = ss + pltpu.roll(ss, 128 - SLOT, 1)
    hi = ss.astype(BF).astype(F32)
    lo = pltpu.roll(ss - hi, SLOT, 1)
    kept = jnp.where(lane < SLOT, hi, jnp.where(lane < 2 * SLOT, lo, 0.0))
    for c in range(4):
        cols = slice(c * 256, c * 256 + 256)
        part = jnp.dot(mine, w_ref[:, cols], preferred_element_type=F32)
        part = part + jnp.dot(other, w_other_ref[:, cols], preferred_element_type=F32)
        if c == 0:
            slot = lax.broadcasted_iota(jnp.int32, ss.shape, 0) % SLOT
            first = jnp.where(slot == SLOT - 1, kept, part[:, :128])
            part = jnp.concatenate([first, part[:, 128:]], axis=1)
        o_ref[:, :, cols] = part.astype(BF).reshape(NZ * NX, SLOT, 256)


def last_kernel(p_ref, x_ref, o_ref):
    lane = lax.broadcasted_iota(jnp.int32, (SLOT, 128), 1)
    slot = lax.broadcasted_iota(jnp.int32, (SLOT, 128), 0)
    mask = (lane == slot) | (lane == slot + SLOT)
    acc = x_ref[...].astype(F32)
    for z in range(NZ):
        part = p_ref[z * NX].astype(F32)
        for x in range(1, NX):
            part = part + p_ref[z * NX + x].astype(F32)
        ss = jnp.broadcast_to(part[SLOT - 1 :, :128], (SLOT, 128))
        ss = jnp.sum(jnp.where(mask, ss, 0.0), axis=1, keepdims=True)
        acc = acc + part * lax.rsqrt(ss / (DI // GROUPS) + EPS)
    o_ref[...] = acc.astype(BF)


def per_device(
    inputs, pre_gain, w_z, w_x, w_bc, w_dt, conv_x_w, conv_bc_w, conv_x_state, conv_bc_state,
    a_log, dt_bias, skip_d, ssm_state, norm_gain, w_out,
):
    core = lax.axis_index("core").astype(jnp.int32).reshape(1)
    w_out_other = swap_core(w_out)
    tokens = jnp.pad(inputs.reshape(STEPS * OWN, -1), ((0, 1), (0, 0)))
    gathered = to_all(tokens, ("z", "x"), NZ * NX)
    other = swap_core(gathered)
    w_small = jnp.concatenate([w_bc, w_dt, jnp.zeros((w_bc.shape[0], 60), BF)], axis=1)
    weights = (pre_gain[None], w_z, w_x, w_small)
    held = project(gathered, *weights, 0)
    pz, px = project(other, *weights, 1, held)

    both = lax.all_to_all(
        jnp.concatenate([pz, px], axis=2), "y", split_axis=0, concat_axis=0, tiled=True
    )
    gate = jnp.sum(both[:, :, :256].astype(F32), axis=0)
    px = both[:, :, 256:]

    cur, rstd, bcc = call(
        shared_kernel,
        (
            jax.ShapeDtypeStruct((STEPS * RB, 384), BF),
            jax.ShapeDtypeStruct((BLOCK, 128), F32),
            jax.ShapeDtypeStruct((STEPS * RB, 64), BF),
        ),
        [SM, VM, VM, VM],
    )(core, px, jnp.swapaxes(conv_bc_state, 0, 1), conv_bc_w)
    vectors = to_all(bcc, ("x", "core"), NX * NC)

    u = call(
        state_kernel,
        jax.ShapeDtypeStruct((BLOCK, 256), BF),
        [SM] * 4 + [VM] * 8,
        scratch_shapes=[pltpu.VMEM((2, RB * 8, 128), F32)] * 2,
    )(
        core, a_log, dt_bias, skip_d, vectors, cur, gate, rstd, jnp.swapaxes(conv_x_state, 0, 1),
        conv_x_w, norm_gain[None], ssm_state.reshape(RB, 256, 256),
    )
    mine = jnp.stack([u[:HALF], swap_core(u[HALF:])], 0)
    rows = to_all(mine, "y", NY)
    partial_sums = call(
        out_kernel, jax.ShapeDtypeStruct((NZ * NX, SLOT, w_out.shape[1]), BF), [VM] * 3
    )(rows, w_out, w_out_other)
    received = lax.all_to_all(partial_sums, ("z", "x"), split_axis=0, concat_axis=0, tiled=True)
    out = call(last_kernel, jax.ShapeDtypeStruct(tokens.shape, BF), [VM] * 2)(received, tokens)
    return out[: STEPS * OWN].reshape(inputs.shape)


def solution(mesh):
    fine = Mesh(mesh.devices.reshape(NZ, NX, NC, NY), (*WIDE, "y"))
    return jax.shard_map(
        per_device,
        mesh=fine,
        in_specs=(
            P(None, WIDE, "y"),
            P("y"),
            P("y", WIDE),
            P("y", WIDE),
            P("y", WIDE),
            P("y", WIDE),
            P(None, WIDE),
            P(None, WIDE),
            P("y", None, WIDE),
            P("y", None, WIDE),
            P(WIDE),
            P(WIDE),
            P(WIDE),
            P("y", WIDE, None, None),
            P(WIDE),
            P(WIDE, "y"),
        ),
        out_specs=P(None, WIDE, "y"),
        check_vma=False,
    )
```

```python
import jax
import jax.numpy as jnp
from jax import lax
from jax.experimental import pallas as pl
from jax.experimental.pallas import tpu as pltpu
from jax.sharding import Mesh
from jax.sharding import PartitionSpec as P

D = 8192
GROUPS = 8
DI = 16384
STEPS = 5
CONVK = 4
EPS = 1e-05

NZ, NX, NC, NY = 8, 4, 2, 8
OWN = 3
SLOT = 16
HALF = NX * SLOT
BLOCK = NC * HALF
RB = 24
BF = jnp.bfloat16
F32 = jnp.float32
WIDE = ("z", "x", "core")


def swap_core(v):
    return lax.ppermute(v, "core", [(0, 1), (1, 0)])


def to_all(v, axes, count):
    return lax.all_to_all(
        jnp.broadcast_to(v[None], (count,) + v.shape), axes, split_axis=0, concat_axis=0, tiled=True
    )


def exchange(v, axes):
    return lax.all_to_all(v, axes, split_axis=0, concat_axis=0, tiled=True)


def call(kernel, out_shape, in_specs, vmem=48, **kw):
    return pl.pallas_call(
        kernel,
        out_shape=out_shape,
        in_specs=in_specs,
        compiler_params=pltpu.CompilerParams(vmem_limit_bytes=vmem * 2**20),
        **kw,
    )


VM = pl.BlockSpec(memory_space=pltpu.VMEM)
SM = pl.BlockSpec(memory_space=pltpu.SMEM)


def scaled_rows(g_ref, gain_ref, x):
    raw = g_ref[x].reshape(NZ * SLOT, -1).astype(F32)
    return raw, (raw * gain_ref[...]).astype(BF)


def over(lhs, w_ref, k):
    return lax.dot_general(lhs, w_ref[...], (((1,), (k,)), ((), ())), preferred_element_type=F32)


def small_kernel(pos_ref, g_ref, gain_ref, *refs):
    weights, out_ref = (refs[:2], refs[2:4]), refs[4]
    core = pos_ref[0]
    for x in range(NX):
        rows = slice(x * SLOT, x * SLOT + SLOT)
        raw, lhs = scaled_rows(g_ref, gain_ref, x)
        ss = jnp.sum(raw * raw, axis=1, keepdims=True)
        hi = ss.astype(BF).astype(F32)
        tail = [hi, ss - hi, jnp.zeros((NZ * SLOT, 58), F32)]
        for to, (wbc_ref, wdt_ref) in zip((core, 1 - core), weights):
            out = jnp.concatenate([over(lhs, wbc_ref, 1), over(lhs, wdt_ref, 1)] + tail, axis=1)
            out_ref[to, :, rows] = out.astype(BF).reshape(NZ, SLOT, 128)


def large_kernel(pos_ref, g_ref, gain_ref, *refs):
    weights, out_ref = (refs[:2], refs[2:4]), refs[4]
    core = pos_ref[0]
    for x in range(NX):
        rows = slice(x * SLOT, x * SLOT + SLOT)
        _, lhs = scaled_rows(g_ref, gain_ref, x)
        for to, pair in zip((core, 1 - core), weights):
            for i, w_ref in enumerate(pair):
                out = over(lhs, w_ref, 0).astype(BF).reshape(NZ, SLOT, 256)
                out_ref[to, :, rows, i * 256 : i * 256 + 256] = out


def slot_of(m):
    core, x, j = m // HALF, m % HALF // SLOT, m % SLOT
    step = (j * 11) // 32
    q = x * NC + core
    return step * RB + q * OWN + (j - step * OWN), j, q


def step_from_slot():
    i = lax.broadcasted_iota(jnp.int32, (STEPS * RB, BLOCK), 0)
    at, j, _ = slot_of(lax.broadcasted_iota(jnp.int32, (STEPS * RB, BLOCK), 1))
    return jnp.where((at == i) & (j < SLOT - 1), 1.0, 0.0).astype(BF)


def slot_from_step():
    shape = (BLOCK, STEPS * RB)
    at, j, q = slot_of(lax.broadcasted_iota(jnp.int32, shape, 0))
    i = lax.broadcasted_iota(jnp.int32, shape, 1)
    row = i % RB
    last = j == SLOT - 1
    order = jnp.where((at == i) & ~last, 1.0, 0.0).astype(BF)
    collect = jnp.where((row // OWN == q) & last, 1.0, 0.0).astype(BF)
    return order, collect


def conv(hist_ref, current, taps):
    seq = [hist_ref[k].astype(F32) for k in range(CONVK - 1)]
    seq += [current[t * RB : (t + 1) * RB] for t in range(STEPS)]
    out = []
    for t in range(STEPS):
        acc = taps[0:1] * seq[t]
        for k in range(1, CONVK):
            acc = acc + taps[k : k + 1] * seq[t + k]
        out.append(acc * jax.nn.sigmoid(acc))
    return out


def summed(p_ref):
    total = []
    for c in range(NC):
        part = p_ref[c * NY].astype(F32)
        for n in range(1, NY):
            part = part + p_ref[c * NY + n].astype(F32)
        total.append(part)
    return jnp.concatenate(total, axis=0)


def shared_kernel(p_ref, hist_ref, taps_ref, cur_ref, bcc_ref):
    total = summed(p_ref)
    rstd = lax.rsqrt((total[:, 68:69] + total[:, 69:70]) / D + EPS)
    lane = lax.broadcasted_iota(jnp.int32, (BLOCK, 128), 1)
    small, rest = total * rstd, rstd
    for k in range(3):
        piece = rest.astype(BF).astype(F32)
        small = jnp.where(lane == 70 + k, piece, small)
        rest = rest - piece
    cur = jnp.dot(step_from_slot(), small.astype(BF), preferred_element_type=F32)
    cur_ref[...] = cur.astype(BF)
    out = conv(hist_ref, cur[:, :64], taps_ref[...]) + [jnp.zeros((8, 64), F32)]
    out = jnp.concatenate(out, axis=0)
    bcc_ref[...] = jnp.concatenate([out[:64], out[64:]], axis=1).astype(BF)


def state_kernel(
    pos_ref, bc_0, bc_1, bc_2, bc_3, cur_ref, p_ref, params_ref, hist_ref, s_ref, u_ref,
    c_rows, y_rows, bc_ref,
):
    at = lambda v, t: v[t * RB : (t + 1) * RB]
    core, here = pos_ref[0], pos_ref[1]
    for shift, ref in enumerate((bc_0, bc_1, bc_2, bc_3)):
        frm = (here + NX - shift) % NX
        bc_ref[frm * NC + core] = ref[0].astype(F32)
        bc_ref[frm * NC + 1 - core] = ref[1].astype(F32)
    bc = [bc_ref[i] for i in range(NX * NC)]
    bc = [jnp.concatenate([v[:, :64], v[:, 64:]], axis=0) for v in bc]
    b_vec = jnp.concatenate(bc[:4], axis=1)
    c_vec = jnp.concatenate(bc[4:], axis=1)

    c_rows[...] = jnp.zeros_like(c_rows)
    for t in range(STEPS):
        for h in range(2):
            c_rows[h, pl.ds(t, RB, stride=8), :] = at(c_vec, t)[:, h * 128 : h * 128 + 128]
    for r in range(RB):
        c_row = jnp.concatenate([c_rows[h, r * 8 : r * 8 + 8, :] for h in range(2)], axis=1)
        y_row = lax.dot_general(
            c_row.astype(BF), s_ref[r], (((1,), (1,)), ((), ())), preferred_element_type=F32
        )
        for h in range(2):
            y_rows[h, r * 8 : r * 8 + 8, :] = y_row[:, h * 128 : h * 128 + 128]

    cur = cur_ref[...]
    taps, gain = params_ref[0:4], params_ref[4:5]
    a_log, bias, skip = params_ref[5:6], params_ref[6:7], params_ref[7:8]
    lane = lax.broadcasted_iota(jnp.int32, (128, 256), 0)
    head = lax.broadcasted_iota(jnp.int32, (128, 256), 1) // 64
    spread = jnp.where(lane == head + 64, 1.0, 0.0).astype(BF)
    dt_raw = jnp.dot(cur, spread, preferred_element_type=F32)
    pre = dt_raw + bias
    dt = jnp.maximum(pre, 0.0) + jnp.log1p(jnp.exp(-jnp.abs(pre)))
    decay = jnp.exp(-dt * jnp.exp(a_log))

    order, collect = slot_from_step()
    rstd = jnp.dot(order, cur, preferred_element_type=F32)
    rstd = rstd[:, 70:71] + rstd[:, 71:72] + rstd[:, 72:73]
    raw = (summed(p_ref) * rstd).astype(BF)
    raw = jnp.dot(step_from_slot(), raw, preferred_element_type=F32)
    gate = raw[:, 256:]
    gate = gate * jax.nn.sigmoid(gate)
    inner = conv(hist_ref, raw[:, :256], taps)
    carried, terms, gated = None, [], []
    for t in range(STEPS):
        d = at(decay, t)
        carried = d if carried is None else carried * d
        terms = [term * d for term in terms] + [at(dt, t) * inner[t]]
        held = [y_rows[h, pl.ds(t, RB, stride=8), :] for h in range(2)]
        y = carried * jnp.concatenate(held, axis=1) + skip * inner[t]
        for s in range(t + 1):
            y = y + jnp.sum(at(c_vec, t) * at(b_vec, s), axis=1, keepdims=True) * terms[s]
        gated.append(y * at(gate, t))
    gated = jnp.concatenate(gated, axis=0)
    ss = jnp.sum(gated * gated, axis=1, keepdims=True)
    hi = ss.astype(BF).astype(F32)
    lo = ss - hi
    row = lax.broadcasted_iota(jnp.int32, gated.shape, 0)
    lane = lax.broadcasted_iota(jnp.int32, gated.shape, 1)
    slot = row // RB * OWN + row % RB % OWN
    sums = jnp.where(lane == slot, hi, jnp.where(lane == slot + SLOT, lo, 0.0)).astype(BF)
    u = jnp.dot(order, (gated * gain).astype(BF), preferred_element_type=F32)
    u = (u + jnp.dot(collect, sums, preferred_element_type=F32)).astype(BF)
    for c in range(NC):
        for n in range(NY):
            u_ref[c * NY + n] = u[c * HALF : c * HALF + HALF]


def out_kernel(pos_ref, u_ref, w_ref, w_other_ref, o_ref):
    core = pos_ref[0]
    slot = lax.broadcasted_iota(jnp.int32, (NY * SLOT, 128), 0) % SLOT
    lane = lax.broadcasted_iota(jnp.int32, (NY * SLOT, 128), 1)
    for x in range(NX):
        rows = slice(x * SLOT, x * SLOT + SLOT)
        mine = u_ref[core, :, rows].reshape(NY * SLOT, 256)
        other = u_ref[1 - core, :, rows].reshape(NY * SLOT, 256)
        ss = mine[:, :128].astype(F32) + other[:, :128].astype(F32)
        ss = ss + pltpu.roll(ss, 128 - SLOT, 1)
        hi = ss.astype(BF).astype(F32)
        lo = pltpu.roll(ss - hi, SLOT, 1)
        kept = jnp.where(lane < SLOT, hi, jnp.where(lane < 2 * SLOT, lo, 0.0))
        for c in range(4):
            cols = slice(c * 256, c * 256 + 256)
            part = jnp.dot(mine, w_ref[:, cols], preferred_element_type=F32)
            part = part + jnp.dot(other, w_other_ref[:, cols], preferred_element_type=F32)
            if c == 0:
                first = jnp.where(slot == SLOT - 1, kept, part[:, :128])
                part = jnp.concatenate([first, part[:, 128:]], axis=1)
            o_ref[x, :, :, cols] = part.astype(BF).reshape(NZ, SLOT, 256)


def group_kernel(p_ref, o_ref):
    lane = lax.broadcasted_iota(jnp.int32, (SLOT, 128), 1)
    slot = lax.broadcasted_iota(jnp.int32, (SLOT, 128), 0)
    mask = (lane == slot) | (lane == slot + SLOT)
    for z in range(NZ):
        part = p_ref[0, z].astype(F32)
        for x in range(1, NX):
            part = part + p_ref[x, z].astype(F32)
        ss = jnp.broadcast_to(part[SLOT - 1 :, :128], (SLOT, 128))
        ss = jnp.sum(jnp.where(mask, ss, 0.0), axis=1, keepdims=True)
        o_ref[z] = (part * lax.rsqrt(ss / (DI // GROUPS) + EPS)).astype(BF)


def last_kernel(p_ref, x_ref, o_ref):
    acc = x_ref[...].astype(F32)
    for z in range(NZ):
        acc = acc + p_ref[z].astype(F32)
    for t in range(STEPS):
        o_ref[t] = acc[t * OWN : t * OWN + OWN].astype(BF)


def per_device(
    inputs, pre_gain, w_z, w_x, w_bc, w_dt, conv_x_w, conv_bc_w, conv_x_state, conv_bc_state,
    a_log, dt_bias, skip_d, ssm_state, norm_gain, w_out,
):
    shape = jax.ShapeDtypeStruct
    pos = jnp.stack([lax.axis_index("core"), lax.axis_index("x")]).astype(jnp.int32)
    narrow, broad = (w_bc.T, w_dt.T), (w_x, w_z)
    tokens = jnp.pad(inputs.reshape(STEPS * OWN, -1), ((0, 1), (0, 0)))
    gathered = to_all(to_all(tokens, "z", NZ), "x", NX)
    pair = lambda ws: (*ws, *(swap_core(w) for w in ws))
    small = call(small_kernel, shape((NC, NY, HALF, 128), BF), [SM] + [VM] * 6)(
        pos, gathered, pre_gain[None], *pair(narrow)
    )
    large = call(large_kernel, shape((NC, NY, HALF, 512), BF), [SM] + [VM] * 6)(
        pos, gathered, pre_gain[None], *pair(broad)
    )
    small, a_log, dt_bias, skip_d, norm_gain, conv_x_w = lax.optimization_barrier(
        (small, a_log, dt_bias, skip_d, norm_gain, conv_x_w)
    )
    heads = jnp.repeat(jnp.stack([a_log, dt_bias, skip_d]), 64, axis=1)
    params = jnp.concatenate([conv_x_w, norm_gain[None], heads], axis=0)

    small = exchange(small.reshape(NC * NY, HALF, 128), ("core", "y"))
    cur, bcc = call(
        shared_kernel, (shape((STEPS * RB, 128), BF), shape((64, 128), BF)), [VM] * 3
    )(small, jnp.swapaxes(conv_bc_state, 0, 1), conv_bc_w)
    large, bcc = lax.optimization_barrier((large, bcc))
    large = exchange(large.reshape(NC * NY, HALF, 512), ("core", "y"))
    vectors = jnp.stack([bcc, swap_core(bcc)])
    vectors = [vectors] + [
        lax.ppermute(vectors, "x", [(i, (i + k) % NX) for i in range(NX)]) for k in range(1, NX)
    ]
    u = call(
        state_kernel,
        shape((NC * NY, HALF, 256), BF),
        [SM] + [VM] * 9,
        scratch_shapes=[pltpu.VMEM((2, RB * 8, 128), F32)] * 2
        + [pltpu.VMEM((NX * NC, 64, 128), F32)],
    )(
        pos, *vectors, cur, large, params, jnp.swapaxes(conv_x_state, 0, 1),
        ssm_state.reshape(RB, 256, 256),
    )
    rows = exchange(u, ("core", "y")).reshape(NC, NY, HALF, 256)
    sums = call(out_kernel, shape((NX, NZ, SLOT, w_out.shape[1]), BF), [SM] + [VM] * 3)(
        pos, rows, w_out, swap_core(w_out)
    )
    sums = call(group_kernel, shape(sums.shape[1:], BF), [VM])(exchange(sums, "x"))
    return call(last_kernel, shape(inputs.shape, BF), [VM] * 2)(exchange(sums, "z"), tokens)


def solution(mesh):
    fine = Mesh(mesh.devices.reshape(NZ, NX, NC, NY), (*WIDE, "y"))
    return jax.shard_map(
        per_device,
        mesh=fine,
        in_specs=(
            P(None, WIDE, "y"),
            P("y"),
            P("y", WIDE),
            P("y", WIDE),
            P("y", WIDE),
            P("y", WIDE),
            P(None, WIDE),
            P(None, WIDE),
            P("y", None, WIDE),
            P("y", None, WIDE),
            P(WIDE),
            P(WIDE),
            P(WIDE),
            P("y", WIDE, None, None),
            P(WIDE),
            P(WIDE, "y"),
        ),
        out_specs=P(None, WIDE, "y"),
        check_vma=False,
    )
```

```python
import jax
import jax.numpy as jnp
from jax import lax
from jax.experimental import pallas as pl
from jax.experimental.pallas import tpu as pltpu
from jax.sharding import Mesh
from jax.sharding import PartitionSpec as P

D = 8192
GROUPS = 8
DI = 16384
STEPS = 5
CONVK = 4
EPS = 1e-05

NZ, NX, NC, NY = 8, 4, 2, 8
OWN = 3
SLOT = 16
HALF = NX * SLOT
BLOCK = NC * HALF
RB = 24
BF = jnp.bfloat16
F32 = jnp.float32
WIDE = ("z", "x", "core")


def swap_core(v):
    return lax.ppermute(v, "core", [(0, 1), (1, 0)])


def to_all(v, axes, count):
    return lax.all_to_all(
        jnp.broadcast_to(v[None], (count,) + v.shape), axes, split_axis=0, concat_axis=0, tiled=True
    )


def around_x(v):
    ways = [[(i, (i + k) % NX) for i in range(NX)] for k in range(1, NX)]
    return [v] + [lax.ppermute(v, "x", way) for way in ways]


def exchange(v, axes):
    return lax.all_to_all(v, axes, split_axis=0, concat_axis=0, tiled=True)


def call(kernel, out_shape, in_specs, vmem=32, **kw):
    return pl.pallas_call(
        kernel,
        out_shape=out_shape,
        in_specs=in_specs,
        compiler_params=pltpu.CompilerParams(vmem_limit_bytes=vmem * 2**20),
        **kw,
    )


VM = pl.BlockSpec(memory_space=pltpu.VMEM)
SM = pl.BlockSpec(memory_space=pltpu.SMEM)


def over(lhs, w, k):
    return lax.dot_general(lhs, w, (((1,), (k,)), ((), ())), preferred_element_type=F32)


def into_empty(values, lanes, rows):
    slot = lax.broadcasted_iota(jnp.int32, rows.shape, 0) % SLOT
    total = jnp.sum(values.reshape(-1, SLOT, 128), axis=1, keepdims=True)
    total = jnp.broadcast_to(total, (rows.shape[0] // SLOT, SLOT, 128)).reshape(rows.shape)
    return jnp.where((slot == SLOT - 1) & lanes, total, rows)


def small_kernel(pos_ref, g_ref, gain_ref, w_ref, w_other_ref, out_ref):
    raw = g_ref[...].reshape(NX * NZ * SLOT, -1).astype(F32)
    lhs = (raw * gain_ref[...]).astype(BF)
    out = over(lhs, jnp.concatenate([w_ref[...], w_other_ref[...]], axis=0), 1)
    ss = jnp.sum(raw * raw, axis=1, keepdims=True)
    hi = ss.astype(BF).astype(F32)
    lane = lax.broadcasted_iota(jnp.int32, out.shape, 1) % 64
    slot = lax.broadcasted_iota(jnp.int32, out.shape, 0) % SLOT
    ss = jnp.where(lane == slot, hi, jnp.where(lane == slot + SLOT, ss - hi, 0.0))
    out = into_empty(ss, lane < 2 * SLOT, out).reshape(NX, NZ, SLOT, 128)
    for x in range(2):
        low, high = out[x], out[x + 2]
        rows = slice(x * SLOT, x * SLOT + SLOT)
        own = jnp.concatenate([low[:, :, :64], high[:, :, :64]], axis=2)
        other = jnp.concatenate([low[:, :, 64:], high[:, :, 64:]], axis=2)
        out_ref[pos_ref[0], :, rows] = own.astype(BF)
        out_ref[1 - pos_ref[0], :, rows] = other.astype(BF)


def large_kernel(pos_ref, g_ref, gain_ref, *refs):
    weights, out_ref = refs[:6], refs[6]
    size = NZ * SLOT
    lhs = (g_ref[...].reshape(NX * size, -1).astype(F32) * gain_ref[...]).astype(BF)
    heads = [
        jnp.broadcast_to(ref[h : h + 1, :].astype(F32), (SLOT, D // NY))
        for ref in weights[4:]
        for h in range(4)
    ]
    sizes = over(lhs, jnp.concatenate(heads, axis=0).astype(BF), 1)
    lane = lax.broadcasted_iota(jnp.int32, sizes.shape, 1)
    slot = lax.broadcasted_iota(jnp.int32, sizes.shape, 0) % SLOT
    sizes = jnp.where(lane % SLOT == slot, sizes, 0.0)
    sizes = (sizes, pltpu.roll(sizes, 64, 1))
    core = pos_ref[0]
    for i, w_ref in enumerate(weights[:4]):
        to, cols = (core, 1 - core)[i // 2], slice(i % 2 * 256, i % 2 * 256 + 256)
        out = jnp.dot(lhs, w_ref[...], preferred_element_type=F32)
        if i % 2 == 0:
            first = into_empty(sizes[i // 2], lane < 64, out[:, :128])
            out = jnp.concatenate([first, out[:, 128:]], axis=1)
        out = out.astype(BF)
        for x in range(NX):
            out_ref[to, :, x * SLOT : x * SLOT + SLOT, cols] = out[
                x * size : x * size + size
            ].reshape(NZ, SLOT, 256)


def slot_of(m):
    core, x, j = m // HALF, m % HALF // SLOT, m % SLOT
    step = (j * 11) // 32
    q = x * NC + core
    return step * RB + q * OWN + (j - step * OWN), j, q


def step_from_slot():
    i = lax.broadcasted_iota(jnp.int32, (STEPS * RB, BLOCK), 0)
    at, j, _ = slot_of(lax.broadcasted_iota(jnp.int32, (STEPS * RB, BLOCK), 1))
    return jnp.where((at == i) & (j < SLOT - 1), 1.0, 0.0).astype(BF)


def slot_from_step():
    shape = (BLOCK, STEPS * RB)
    at, j, q = slot_of(lax.broadcasted_iota(jnp.int32, shape, 0))
    i = lax.broadcasted_iota(jnp.int32, shape, 1)
    row = i % RB
    last = j == SLOT - 1
    order = jnp.where((at == i) & ~last, 1.0, 0.0).astype(BF)
    collect = jnp.where((row // OWN == q) & last, 1.0, 0.0).astype(BF)
    return order, collect


def conv(hist_ref, current, taps):
    seq = [hist_ref[k].astype(F32) for k in range(CONVK - 1)]
    seq += [current[t * RB : (t + 1) * RB] for t in range(STEPS)]
    out = []
    for t in range(STEPS):
        acc = taps[0:1] * seq[t]
        for k in range(1, CONVK):
            acc = acc + taps[k : k + 1] * seq[t + k]
        out.append(acc * jax.nn.sigmoid(acc))
    return out


def empty_sums(rows):
    slot = lax.broadcasted_iota(jnp.int32, rows.shape, 0) % SLOT
    lane = lax.broadcasted_iota(jnp.int32, rows.shape, 1)
    mask = (lane == slot) | (lane == slot + SLOT)
    shape = (rows.shape[0] // SLOT, SLOT, rows.shape[1])
    ss = jnp.broadcast_to(rows.reshape(shape)[:, SLOT - 1 :], shape).reshape(rows.shape)
    return jnp.sum(jnp.where(mask, ss, 0.0), axis=1, keepdims=True)


def shared_kernel(p_ref, hist_ref, taps_ref, rstd_ref, bcc_ref):
    total = []
    for c in range(NC):
        part = p_ref[c * NY].astype(F32)
        for n in range(1, NY):
            part = part + p_ref[c * NY + n].astype(F32)
        total += [part[:, :64], part[:, 64:]]
    total = jnp.concatenate(total, axis=0)
    rest = rstd = lax.rsqrt(empty_sums(total) / D + EPS)
    lane = lax.broadcasted_iota(jnp.int32, total.shape, 1)
    factor = jnp.zeros(total.shape, F32)
    for k in range(3):
        piece = rest.astype(BF).astype(F32)
        factor = jnp.where(lane == k, piece, factor)
        rest = rest - piece
    raw = jnp.concatenate([total * rstd, factor], axis=1).astype(BF)
    cur = jnp.dot(step_from_slot(), raw, preferred_element_type=F32)
    rstd = cur[:, 64:65] + cur[:, 65:66] + cur[:, 66:67]
    rstd_ref[...] = jnp.broadcast_to(rstd, rstd_ref.shape)
    out = conv(hist_ref, cur[:, :64], taps_ref[...]) + [jnp.zeros((8, 64), F32)]
    out = jnp.concatenate(out, axis=0)
    bcc_ref[...] = jnp.concatenate([out[:64], out[64:]], axis=1).astype(BF)


def at(v, t):
    return v[t * RB : (t + 1) * RB]


def carried_kernel(
    pos_ref, bc_0, bc_1, bc_2, bc_3, rstd_ref, s_ref, y_ref, pairs_ref, sum_ref, empty_ref,
    c_rows, y_rows, held,
):
    core, here = pos_ref[0], pos_ref[1]
    for k, ref in enumerate((bc_0, bc_1, bc_2, bc_3)):
        frm = (here + NX - k) % NX
        held[frm * NC + core] = ref[0].astype(F32)
        held[frm * NC + 1 - core] = ref[1].astype(F32)
    vectors = [held[i] for i in range(NX * NC)]
    vectors = [jnp.concatenate([v[:, :64], v[:, 64:]], axis=0) for v in vectors]
    b_vec = jnp.concatenate(vectors[:4], axis=1)
    c_vec = jnp.concatenate(vectors[4:], axis=1)

    c_rows[...] = jnp.zeros_like(c_rows)
    for t in range(STEPS):
        for h in range(2):
            c_rows[h, pl.ds(t, RB, stride=8), :] = at(c_vec, t)[:, h * 128 : h * 128 + 128]
    for r in range(RB):
        c_row = jnp.concatenate([c_rows[h, r * 8 : r * 8 + 8, :] for h in range(2)], axis=1)
        y_row = lax.dot_general(
            c_row.astype(BF), s_ref[r], (((1,), (1,)), ((), ())), preferred_element_type=F32
        )
        for h in range(2):
            y_rows[h, r * 8 : r * 8 + 8, :] = y_row[:, h * 128 : h * 128 + 128]

    for t in range(STEPS):
        for h in range(2):
            y_ref[t * RB : t * RB + RB, h * 128 : h * 128 + 128] = y_rows[h, pl.ds(t, RB, stride=8), :]
    rstd = rstd_ref[...]
    lane = lax.broadcasted_iota(jnp.int32, (RB, 128), 1)
    for t in range(STEPS):
        out = at(rstd, t)
        for s in range(t + 1):
            pair = jnp.sum(at(c_vec, t) * at(b_vec, s), axis=1, keepdims=True)
            out = jnp.where(lane == s, pair, out)
        pairs_ref[t * RB : t * RB + RB, :] = out
    m = lax.broadcasted_iota(jnp.int32, (1, NC * NY * HALF), 1)
    x, j = m % HALF // SLOT, m % SLOT
    q = x * NC + m // (NY * HALF)
    step = (j * 11) // 32
    row = jnp.where(j < SLOT - 1, step * RB + q * OWN + j - step * OWN, -1)
    i = lax.broadcasted_iota(jnp.int32, (STEPS * RB, 1), 0)
    sum_ref[...] = jnp.where(row == i, 1.0, 0.0).astype(BF)
    q = jnp.where(j == SLOT - 1, q, -1)
    empty_ref[...] = jnp.where(q == i % RB // OWN, 1.0, 0.0).astype(BF)


def state_kernel(y0_ref, pairs_ref, sum_ref, empty_ref, p_ref, params_ref, hist_ref, u_ref):
    taps, gain = params_ref[0:4], params_ref[4:5]
    a_log, bias, skip = params_ref[5:6], params_ref[6:7], params_ref[7:8]
    pairs = pairs_ref[...]
    rstd = pairs[:, 127:]
    large = p_ref[...].reshape(NC * NY * HALF, 512)
    sizes = jnp.dot(empty_ref[...], large[:, :128], preferred_element_type=F32) * rstd
    row = lax.broadcasted_iota(jnp.int32, sizes.shape, 0)
    lane = lax.broadcasted_iota(jnp.int32, sizes.shape, 1)
    slot = row // RB * OWN + row % RB % OWN
    sizes = jnp.where((lane % SLOT == slot) & (lane < 64), sizes, 0.0).astype(BF)
    lane = lax.broadcasted_iota(jnp.int32, (128, 256), 0)
    head = lax.broadcasted_iota(jnp.int32, (128, 256), 1) // 64
    spread = jnp.where(lane // SLOT == head, 1.0, 0.0).astype(BF)
    pre = jnp.dot(sizes, spread, preferred_element_type=F32) + bias
    dt = jnp.maximum(pre, 0.0) + jnp.log1p(jnp.exp(-jnp.abs(pre)))
    decay = jnp.exp(-dt * jnp.exp(a_log))
    order, collect = slot_from_step()
    raw = jnp.dot(sum_ref[...], large, preferred_element_type=F32) * rstd
    raw = raw.astype(BF).astype(F32)
    gate = raw[:, 256:]
    gate = gate * jax.nn.sigmoid(gate)
    inner = conv(hist_ref, raw[:, :256], taps)
    carried, terms, gated = None, [], []
    for t in range(STEPS):
        d = at(decay, t)
        carried = d if carried is None else carried * d
        terms = [term * d for term in terms] + [at(dt, t) * inner[t]]
        y = carried * at(y0_ref, t) + skip * inner[t]
        for s in range(t + 1):
            y = y + at(pairs, t)[:, s : s + 1] * terms[s]
        gated.append(y * at(gate, t))
    gated = jnp.concatenate(gated, axis=0)
    ss = jnp.sum(gated * gated, axis=1, keepdims=True)
    hi = ss.astype(BF).astype(F32)
    lo = ss - hi
    row = lax.broadcasted_iota(jnp.int32, gated.shape, 0)
    lane = lax.broadcasted_iota(jnp.int32, gated.shape, 1)
    slot = row // RB * OWN + row % RB % OWN
    sums = jnp.where(lane == slot, hi, jnp.where(lane == slot + SLOT, lo, 0.0)).astype(BF)
    u = jnp.dot(order, (gated * gain).astype(BF), preferred_element_type=F32)
    u = (u + jnp.dot(collect, sums, preferred_element_type=F32)).astype(BF)
    for c in range(NC):
        for n in range(NY):
            u_ref[c * NY + n] = u[c * HALF : c * HALF + HALF]


def out_kernel(pos_ref, u_ref, w_ref, w_other_ref, o_ref):
    core = pos_ref[0]
    slot = lax.broadcasted_iota(jnp.int32, (NY * SLOT, 128), 0) % SLOT
    lane = lax.broadcasted_iota(jnp.int32, (NY * SLOT, 128), 1)
    for x in range(NX):
        rows = slice(x * SLOT, x * SLOT + SLOT)
        mine = u_ref[core, :, rows].reshape(NY * SLOT, 256)
        other = u_ref[1 - core, :, rows].reshape(NY * SLOT, 256)
        ss = mine[:, :128].astype(F32) + other[:, :128].astype(F32)
        ss = ss + pltpu.roll(ss, 128 - SLOT, 1)
        hi = ss.astype(BF).astype(F32)
        lo = pltpu.roll(ss - hi, SLOT, 1)
        kept = jnp.where(lane < SLOT, hi, jnp.where(lane < 2 * SLOT, lo, 0.0))
        for c in range(4):
            cols = slice(c * 256, c * 256 + 256)
            part = jnp.dot(mine, w_ref[:, cols], preferred_element_type=F32)
            part = part + jnp.dot(other, w_other_ref[:, cols], preferred_element_type=F32)
            if c == 0:
                first = jnp.where(slot == SLOT - 1, kept, part[:, :128])
                part = jnp.concatenate([first, part[:, 128:]], axis=1)
            o_ref[x, :, :, cols] = part.astype(BF).reshape(NZ, SLOT, 256)


def group_kernel(p_ref, o_ref):
    for z in range(NZ):
        part = p_ref[0, z].astype(F32)
        for x in range(1, NX):
            part = part + p_ref[x, z].astype(F32)
        scale = lax.rsqrt(empty_sums(part[:, :128]) / (DI // GROUPS) + EPS)
        o_ref[z] = (part * scale).astype(BF)


def last_kernel(p_ref, x_ref, o_ref):
    acc = x_ref[...].astype(F32)
    for z in range(NZ):
        acc = acc + p_ref[z].astype(F32)
    for t in range(STEPS):
        o_ref[t] = acc[t * OWN : t * OWN + OWN].astype(BF)


def per_device(
    inputs, pre_gain, w_z, w_x, w_bc, w_dt, conv_x_w, conv_bc_w, conv_x_state, conv_bc_state,
    a_log, dt_bias, skip_d, ssm_state, norm_gain, w_out,
):
    shape = jax.ShapeDtypeStruct
    pos = jnp.stack([lax.axis_index("core"), lax.axis_index("x")]).astype(jnp.int32)
    tokens = jnp.pad(inputs.reshape(STEPS * OWN, -1), ((0, 1), (0, 0)))
    gathered = to_all(to_all(tokens, "z", NZ), "x", NX)
    gain, w_bc, w_dt = pre_gain[None], w_bc.T, w_dt.T
    small = call(small_kernel, shape((NC, NY, HALF // 2, 128), BF), [SM] + [VM] * 4)(
        pos, gathered, gain, w_bc, swap_core(w_bc)
    )
    weights = (w_x, w_z, swap_core(w_x), swap_core(w_z), w_dt, swap_core(w_dt))
    large = call(large_kernel, shape((NC, NY, HALF, 512), BF), [SM] + [VM] * 8)(
        pos, gathered, gain, *weights
    )
    small, a_log, dt_bias, skip_d, norm_gain, conv_x_w = lax.optimization_barrier(
        (small, a_log, dt_bias, skip_d, norm_gain, conv_x_w)
    )
    heads = jnp.repeat(jnp.stack([a_log, dt_bias, skip_d]), 64, axis=1)
    params = jnp.concatenate([conv_x_w, norm_gain[None], heads], axis=0)

    small = exchange(small.reshape(NC * NY, HALF // 2, 128), ("core", "y"))
    rstd, bcc = call(
        shared_kernel, (shape((STEPS * RB, 128), F32), shape((64, 128), BF)), [VM] * 3
    )(small, jnp.swapaxes(conv_bc_state, 0, 1), conv_bc_w)
    large, bcc = lax.optimization_barrier((large, bcc))
    large = exchange(large.reshape(NC * NY, HALF, 512), ("core", "y"))
    ready = call(
        carried_kernel,
        (
            shape((STEPS * RB, 256), F32),
            shape((STEPS * RB, 128), F32),
            shape((STEPS * RB, NC * NY * HALF), BF),
            shape((STEPS * RB, NC * NY * HALF), BF),
        ),
        [SM] + [VM] * 6,
        scratch_shapes=[pltpu.VMEM((2, RB * 8, 128), F32)] * 2
        + [pltpu.VMEM((NX * NC, 64, 128), F32)],
    )(
        pos, *around_x(jnp.stack([bcc, swap_core(bcc)])), rstd, ssm_state.reshape(RB, 256, 256)
    )
    u = call(state_kernel, shape((NC * NY, HALF, 256), BF), [VM] * 7)(
        *ready, large, params, jnp.swapaxes(conv_x_state, 0, 1)
    )
    rows = exchange(u, ("core", "y")).reshape(NC, NY, HALF, 256)
    sums = call(out_kernel, shape((NX, NZ, SLOT, w_out.shape[1]), BF), [SM] + [VM] * 3)(
        pos, rows, w_out, swap_core(w_out)
    )
    sums = call(group_kernel, shape(sums.shape[1:], BF), [VM])(exchange(sums, "x"))
    return call(last_kernel, shape(inputs.shape, BF), [VM] * 2)(exchange(sums, "z"), tokens)


def solution(mesh):
    fine = Mesh(mesh.devices.reshape(NZ, NX, NC, NY), (*WIDE, "y"))
    return jax.shard_map(
        per_device,
        mesh=fine,
        in_specs=(
            P(None, WIDE, "y"),
            P("y"),
            P("y", WIDE),
            P("y", WIDE),
            P("y", WIDE),
            P("y", WIDE),
            P(None, WIDE),
            P(None, WIDE),
            P("y", None, WIDE),
            P("y", None, WIDE),
            P(WIDE),
            P(WIDE),
            P(WIDE),
            P("y", WIDE, None, None),
            P(WIDE),
            P(WIDE, "y"),
        ),
        out_specs=P(None, WIDE, "y"),
        check_vma=False,
    )
```

```python
import functools

import jax
import jax.numpy as jnp
from jax import lax
from jax.experimental import pallas as pl
from jax.experimental.pallas import tpu as pltpu
from jax.sharding import Mesh
from jax.sharding import PartitionSpec as P

D = 8192
GROUPS = 8
DI = 16384
STEPS = 5
CONVK = 4
EPS = 1e-05

NZ, NX, NC, NY = 8, 4, 2, 8
OWN = 3
SLOT = 16
HALF = NX * SLOT
BLOCK = NC * HALF
RB = 24
BF = jnp.bfloat16
F32 = jnp.float32
WIDE = ("z", "x", "core")


def swap_core(v):
    return lax.ppermute(v, "core", [(0, 1), (1, 0)])


def to_all(v, axes, count):
    return lax.all_to_all(
        jnp.broadcast_to(v[None], (count,) + v.shape), axes, split_axis=0, concat_axis=0, tiled=True
    )


NEXT, ACROSS, PREVIOUS = ([(i, (i + k) % NX) for i in range(NX)] for k in (1, 2, 3))


def around_x(v):
    return [v] + [lax.ppermute(v, "x", way) for way in (NEXT, ACROSS, PREVIOUS)]


def exchange(v, axes):
    return lax.all_to_all(v, axes, split_axis=0, concat_axis=0, tiled=True)


def call(kernel, out_shape, in_specs, vmem=32, **kw):
    return pl.pallas_call(
        kernel,
        out_shape=out_shape,
        in_specs=in_specs,
        compiler_params=pltpu.CompilerParams(vmem_limit_bytes=vmem * 2**20),
        **kw,
    )


VM = pl.BlockSpec(memory_space=pltpu.VMEM)
SM = pl.BlockSpec(memory_space=pltpu.SMEM)


def over(lhs, w, k):
    return lax.dot_general(lhs, w, (((1,), (k,)), ((), ())), preferred_element_type=F32)


def into_empty(values, lanes, rows):
    slot = lax.broadcasted_iota(jnp.int32, rows.shape, 0) % SLOT
    total = jnp.sum(values.reshape(-1, SLOT, 128), axis=1, keepdims=True)
    total = jnp.broadcast_to(total, (rows.shape[0] // SLOT, SLOT, 128)).reshape(rows.shape)
    return jnp.where((slot == SLOT - 1) & lanes, total, rows)


def small_kernel(pos_ref, g_ref, gain_ref, w_ref, w_other_ref, out_ref):
    raw = g_ref[...].reshape(NX * NZ * SLOT, -1).astype(F32)
    lhs = (raw * gain_ref[...]).astype(BF)
    out = over(lhs, jnp.concatenate([w_ref[...], w_other_ref[...]], axis=0), 1)
    ss = jnp.sum(raw * raw, axis=1, keepdims=True)
    hi = ss.astype(BF).astype(F32)
    lane = lax.broadcasted_iota(jnp.int32, out.shape, 1) % 64
    slot = lax.broadcasted_iota(jnp.int32, out.shape, 0) % SLOT
    ss = jnp.where(lane == slot, hi, jnp.where(lane == slot + SLOT, ss - hi, 0.0))
    out = into_empty(ss, lane < 2 * SLOT, out).reshape(NX, NZ, SLOT, 128)
    for x in range(2):
        low, high = out[x], out[x + 2]
        rows = slice(x * SLOT, x * SLOT + SLOT)
        own = jnp.concatenate([low[:, :, :64], high[:, :, :64]], axis=2)
        other = jnp.concatenate([low[:, :, 64:], high[:, :, 64:]], axis=2)
        out_ref[pos_ref[0], :, rows] = own.astype(BF)
        out_ref[1 - pos_ref[0], :, rows] = other.astype(BF)


def large_kernel(pos_ref, g_ref, gain_ref, *refs):
    weights, out_ref = refs[:6], refs[6]
    size = NZ * SLOT
    lhs = (g_ref[...].reshape(NX * size, -1).astype(F32) * gain_ref[...]).astype(BF)
    heads = [
        jnp.broadcast_to(ref[h : h + 1, :].astype(F32), (SLOT, D // NY))
        for ref in weights[4:]
        for h in range(4)
    ]
    sizes = over(lhs, jnp.concatenate(heads, axis=0).astype(BF), 1)
    lane = lax.broadcasted_iota(jnp.int32, sizes.shape, 1)
    slot = lax.broadcasted_iota(jnp.int32, sizes.shape, 0) % SLOT
    sizes = jnp.where(lane % SLOT == slot, sizes, 0.0)
    sizes = (sizes, pltpu.roll(sizes, 64, 1))
    core = pos_ref[0]
    for i, w_ref in enumerate(weights[:4]):
        to, cols = (core, 1 - core)[i // 2], slice(i % 2 * 256, i % 2 * 256 + 256)
        out = jnp.dot(lhs, w_ref[...], preferred_element_type=F32)
        if i % 2 == 0:
            first = into_empty(sizes[i // 2], lane < 64, out[:, :128])
            out = jnp.concatenate([first, out[:, 128:]], axis=1)
        out = out.astype(BF)
        for x in range(NX):
            out_ref[to, :, x * SLOT : x * SLOT + SLOT, cols] = out[
                x * size : x * size + size
            ].reshape(NZ, SLOT, 256)


def slot_of(m):
    core, x, j = m // HALF, m % HALF // SLOT, m % SLOT
    step = (j * 11) // 32
    q = x * NC + core
    return step * RB + q * OWN + (j - step * OWN), j, q


def step_from_slot():
    i = lax.broadcasted_iota(jnp.int32, (STEPS * RB, BLOCK), 0)
    at, j, _ = slot_of(lax.broadcasted_iota(jnp.int32, (STEPS * RB, BLOCK), 1))
    return jnp.where((at == i) & (j < SLOT - 1), 1.0, 0.0).astype(BF)


def slot_from_step():
    shape = (BLOCK, STEPS * RB)
    at, j, q = slot_of(lax.broadcasted_iota(jnp.int32, shape, 0))
    i = lax.broadcasted_iota(jnp.int32, shape, 1)
    row = i % RB
    last = j == SLOT - 1
    order = jnp.where((at == i) & ~last, 1.0, 0.0).astype(BF)
    collect = jnp.where((row // OWN == q) & last, 1.0, 0.0).astype(BF)
    return order, collect


def conv(hist_ref, current, taps):
    seq = [hist_ref[k].astype(F32) for k in range(CONVK - 1)]
    seq += [current[t * RB : (t + 1) * RB] for t in range(STEPS)]
    out = []
    for t in range(STEPS):
        acc = taps[0:1] * seq[t]
        for k in range(1, CONVK):
            acc = acc + taps[k : k + 1] * seq[t + k]
        out.append(acc * jax.nn.sigmoid(acc))
    return out


def empty_sums(rows):
    slot = lax.broadcasted_iota(jnp.int32, rows.shape, 0) % SLOT
    lane = lax.broadcasted_iota(jnp.int32, rows.shape, 1)
    mask = (lane == slot) | (lane == slot + SLOT)
    shape = (rows.shape[0] // SLOT, SLOT, rows.shape[1])
    ss = jnp.broadcast_to(rows.reshape(shape)[:, SLOT - 1 :], shape).reshape(rows.shape)
    return jnp.sum(jnp.where(mask, ss, 0.0), axis=1, keepdims=True)


def shared_kernel(p_ref, hist_ref, taps_ref, rstd_ref, bcc_ref):
    total = []
    for c in range(NC):
        part = p_ref[c * NY].astype(F32)
        for n in range(1, NY):
            part = part + p_ref[c * NY + n].astype(F32)
        total += [part[:, :64], part[:, 64:]]
    total = jnp.concatenate(total, axis=0)
    rest = rstd = lax.rsqrt(empty_sums(total) / D + EPS)
    lane = lax.broadcasted_iota(jnp.int32, total.shape, 1)
    factor = jnp.zeros(total.shape, F32)
    for k in range(3):
        piece = rest.astype(BF).astype(F32)
        factor = jnp.where(lane == k, piece, factor)
        rest = rest - piece
    raw = jnp.concatenate([total * rstd, factor], axis=1).astype(BF)
    cur = jnp.dot(step_from_slot(), raw, preferred_element_type=F32)
    rstd = cur[:, 64:65] + cur[:, 65:66] + cur[:, 66:67]
    rstd_ref[...] = jnp.broadcast_to(rstd, rstd_ref.shape)
    out = conv(hist_ref, cur[:, :64], taps_ref[...]) + [jnp.zeros((8, 64), F32)]
    out = jnp.concatenate(out, axis=0)
    bcc_ref[...] = jnp.concatenate([out[:64], out[64:]], axis=1).astype(BF)


def at(v, t):
    return v[t * RB : (t + 1) * RB]


def carried_kernel(
    pos_ref, bc_0, bc_1, bc_2, bc_3, rstd_ref, s_ref, out_ref, c_rows, y_rows, held
):
    core, here = pos_ref[0], pos_ref[1]
    for k, ref in enumerate((bc_0, bc_1, bc_2, bc_3)):
        frm = (here + NX - k) % NX
        held[frm * NC + core] = ref[0].astype(F32)
        held[frm * NC + 1 - core] = ref[1].astype(F32)
    vectors = [held[i] for i in range(NX * NC)]
    vectors = [jnp.concatenate([v[:, :64], v[:, 64:]], axis=0) for v in vectors]
    b_vec = jnp.concatenate(vectors[:4], axis=1)
    c_vec = jnp.concatenate(vectors[4:], axis=1)

    c_rows[...] = jnp.zeros_like(c_rows)
    for t in range(STEPS):
        for h in range(2):
            c_rows[h, pl.ds(t, RB, stride=8), :] = at(c_vec, t)[:, h * 128 : h * 128 + 128]
    for r in range(RB):
        c_row = jnp.concatenate([c_rows[h, r * 8 : r * 8 + 8, :] for h in range(2)], axis=1)
        y_row = lax.dot_general(
            c_row.astype(BF), s_ref[r], (((1,), (1,)), ((), ())), preferred_element_type=F32
        )
        for h in range(2):
            y_rows[h, r * 8 : r * 8 + 8, :] = y_row[:, h * 128 : h * 128 + 128]

    for t in range(STEPS):
        for h in range(2):
            out_ref[t * RB : t * RB + RB, h * 128 : h * 128 + 128] = y_rows[h, pl.ds(t, RB, stride=8), :]
    rstd = rstd_ref[...]
    lane = lax.broadcasted_iota(jnp.int32, (RB, 128), 1)
    for t in range(STEPS):
        out = at(rstd, t)
        for s in range(t + 1):
            pair = jnp.sum(at(c_vec, t) * at(b_vec, s), axis=1, keepdims=True)
            out = jnp.where(lane == s, pair, out)
        out_ref[t * RB : t * RB + RB, 256:] = out


def state_kernel(ready_ref, p_ref, params_ref, hist_ref, u_ref):
    m = lax.broadcasted_iota(jnp.int32, (1, NC * NY * HALF), 1)
    x, j = m % HALF // SLOT, m % SLOT
    q = x * NC + m // (NY * HALF)
    step = (j * 11) // 32
    row = jnp.where(j < SLOT - 1, step * RB + q * OWN + j - step * OWN, -1)
    i = lax.broadcasted_iota(jnp.int32, (STEPS * RB, 1), 0)
    gather = jnp.where(row == i, 1.0, 0.0).astype(BF)
    q = jnp.where(j == SLOT - 1, q, -1)
    empty = jnp.where(q == i % RB // OWN, 1.0, 0.0).astype(BF)
    taps, gain = params_ref[0:4], params_ref[4:5]
    a_log, bias, skip = params_ref[5:6], params_ref[6:7], params_ref[7:8]
    y0, pairs = ready_ref[:, :256], ready_ref[:, 256:]
    rstd = pairs[:, 127:]
    large = p_ref[...].reshape(NC * NY * HALF, 512)
    sizes = jnp.dot(empty, large[:, :128], preferred_element_type=F32) * rstd
    row = lax.broadcasted_iota(jnp.int32, sizes.shape, 0)
    lane = lax.broadcasted_iota(jnp.int32, sizes.shape, 1)
    slot = row // RB * OWN + row % RB % OWN
    sizes = jnp.where((lane % SLOT == slot) & (lane < 64), sizes, 0.0).astype(BF)
    lane = lax.broadcasted_iota(jnp.int32, (128, 256), 0)
    head = lax.broadcasted_iota(jnp.int32, (128, 256), 1) // 64
    spread = jnp.where(lane // SLOT == head, 1.0, 0.0).astype(BF)
    pre = jnp.dot(sizes, spread, preferred_element_type=F32) + bias
    dt = jnp.maximum(pre, 0.0) + jnp.log1p(jnp.exp(-jnp.abs(pre)))
    decay = jnp.exp(-dt * jnp.exp(a_log))
    order, collect = slot_from_step()
    raw = jnp.dot(gather, large, preferred_element_type=F32) * rstd
    raw = raw.astype(BF).astype(F32)
    gate = raw[:, 256:]
    gate = gate * jax.nn.sigmoid(gate)
    inner = conv(hist_ref, raw[:, :256], taps)
    carried, terms, gated = None, [], []
    for t in range(STEPS):
        d = at(decay, t)
        carried = d if carried is None else carried * d
        terms = [term * d for term in terms] + [at(dt, t) * inner[t]]
        y = carried * at(y0, t) + skip * inner[t]
        for s in range(t + 1):
            y = y + at(pairs, t)[:, s : s + 1] * terms[s]
        gated.append(y * at(gate, t))
    gated = jnp.concatenate(gated, axis=0)
    ss = jnp.sum(gated * gated, axis=1, keepdims=True)
    hi = ss.astype(BF).astype(F32)
    lo = ss - hi
    row = lax.broadcasted_iota(jnp.int32, gated.shape, 0)
    lane = lax.broadcasted_iota(jnp.int32, gated.shape, 1)
    slot = row // RB * OWN + row % RB % OWN
    sums = jnp.where(lane == slot, hi, jnp.where(lane == slot + SLOT, lo, 0.0)).astype(BF)
    u = jnp.dot(order, (gated * gain).astype(BF), preferred_element_type=F32)
    u = (u + jnp.dot(collect, sums, preferred_element_type=F32)).astype(BF)
    for x in range(NX):
        for c in range(NC):
            first = c * HALF + x * SLOT
            for n in range(NY):
                u_ref[x, n, c] = u[first : first + SLOT]


def out_kernel(own, pos_ref, u_ref, w_ref, left_ref, low_ref, high_ref, right_ref, o_ref):
    core, here = pos_ref[0], pos_ref[1]
    which = core if own else 1 - core
    rows = [
        u_ref[(here + NX - k) % NX, :, which].reshape(NY * SLOT, 256) for k in range(NX)
    ]
    ss = rows[0][:, :128].astype(F32)
    for r in rows[1:]:
        ss = ss + r[:, :128].astype(F32)
    if not own:
        lane = lax.broadcasted_iota(jnp.int32, ss.shape, 1)
        ss = ss + pltpu.roll(ss, 128 - SLOT, 1)
        hi = ss.astype(BF).astype(F32)
        lo = pltpu.roll(ss - hi, SLOT, 1)
        ss = jnp.where(lane < SLOT, hi, jnp.where(lane < 2 * SLOT, lo, 0.0))
    dot = lambda v, w: jnp.dot(v, w[...], preferred_element_type=F32)
    total = dot(rows[0], w_ref) + dot(rows[1], left_ref) + dot(rows[3], right_ref)
    total = total + dot(rows[2][:, :128], low_ref) + dot(rows[2][:, 128:], high_ref)
    slot = lax.broadcasted_iota(jnp.int32, ss.shape, 0) % SLOT
    first = jnp.where(slot == SLOT - 1, ss, total[:, :128])
    total = jnp.concatenate([first, total[:, 128:]], axis=1)
    o_ref[...] = total.astype(o_ref.dtype).reshape(o_ref.shape)


def group_kernel(own_ref, other_ref, o_ref):
    total = own_ref[...] + other_ref[...].reshape(NZ * SLOT, -1).astype(F32)
    total = total * lax.rsqrt(empty_sums(total[:, :128]) / (DI // GROUPS) + EPS)
    o_ref[...] = total.astype(BF).reshape(o_ref.shape)


def last_kernel(p_ref, x_ref, o_ref):
    acc = x_ref[...].astype(F32)
    for z in range(NZ):
        acc = acc + p_ref[z].astype(F32)
    for t in range(STEPS):
        o_ref[t] = acc[t * OWN : t * OWN + OWN].astype(BF)


def per_device(
    inputs, pre_gain, w_z, w_x, w_bc, w_dt, conv_x_w, conv_bc_w, conv_x_state, conv_bc_state,
    a_log, dt_bias, skip_d, ssm_state, norm_gain, w_out,
):
    shape = jax.ShapeDtypeStruct
    pos = jnp.stack([lax.axis_index("core"), lax.axis_index("x")]).astype(jnp.int32)
    tokens = jnp.pad(inputs.reshape(STEPS * OWN, -1), ((0, 1), (0, 0)))
    gathered = to_all(to_all(tokens, "z", NZ), "x", NX)
    gain, w_bc, w_dt = pre_gain[None], w_bc.T, w_dt.T
    small = call(small_kernel, shape((NC, NY, HALF // 2, 128), BF), [SM] + [VM] * 4)(
        pos, gathered, gain, w_bc, swap_core(w_bc)
    )
    weights = (w_x, w_z, swap_core(w_x), swap_core(w_z), w_dt, swap_core(w_dt))
    large = call(large_kernel, shape((NC, NY, HALF, 512), BF), [SM] + [VM] * 8)(
        pos, gathered, gain, *weights
    )
    small, a_log, dt_bias, skip_d, norm_gain, conv_x_w = lax.optimization_barrier(
        (small, a_log, dt_bias, skip_d, norm_gain, conv_x_w)
    )
    heads = jnp.repeat(jnp.stack([a_log, dt_bias, skip_d]), 64, axis=1)
    params = jnp.concatenate([conv_x_w, norm_gain[None], heads], axis=0)

    small = exchange(small.reshape(NC * NY, HALF // 2, 128), ("core", "y"))
    rstd, bcc = call(
        shared_kernel, (shape((STEPS * RB, 128), F32), shape((64, 128), BF)), [VM] * 3
    )(small, jnp.swapaxes(conv_bc_state, 0, 1), conv_bc_w)
    large, bcc, w_out = lax.optimization_barrier((large, bcc, w_out))
    left, right = (lax.ppermute(w_out, "x", way) for way in (NEXT, PREVIOUS))
    large = exchange(large.reshape(NC * NY, HALF, 512), ("core", "y"))
    ready = call(
        carried_kernel,
        shape((STEPS * RB, 384), F32),
        [SM] + [VM] * 6,
        scratch_shapes=[pltpu.VMEM((2, RB * 8, 128), F32)] * 2
        + [pltpu.VMEM((NX * NC, 64, 128), F32)],
    )(
        pos, *around_x(jnp.stack([bcc, swap_core(bcc)])), rstd, ssm_state.reshape(RB, 256, 256)
    )
    ready, left, right = lax.optimization_barrier((ready, left, right))
    u = call(state_kernel, shape((NX, NY, NC, SLOT, 256), BF), [VM] * 4)(
        ready, large, params, jnp.swapaxes(conv_x_state, 0, 1)
    )
    u = exchange(u.reshape(NX * NY, NC, SLOT, 256), ("x", "y")).reshape(u.shape)
    half = w_out.shape[0] // 2
    low = lax.ppermute(left[:half], "x", NEXT)
    high = lax.ppermute(right[half:], "x", PREVIOUS)
    width = w_out.shape[1]
    out = lambda own, result: call(
        functools.partial(out_kernel, own), result, [SM] + [VM] * 6
    )(pos, u, w_out, left, low, high, right)
    other = swap_core(out(False, shape((NZ, SLOT, width), BF)))
    sums = call(group_kernel, shape((NZ, SLOT, width), BF), [VM] * 2)(
        out(True, shape((NZ * SLOT, width), F32)), other
    )
    return call(last_kernel, shape(inputs.shape, BF), [VM] * 2)(exchange(sums, "z"), tokens)


def solution(mesh):
    fine = Mesh(mesh.devices.reshape(NZ, NX, NC, NY), (*WIDE, "y"))
    return jax.shard_map(
        per_device,
        mesh=fine,
        in_specs=(
            P(None, WIDE, "y"),
            P("y"),
            P("y", WIDE),
            P("y", WIDE),
            P("y", WIDE),
            P("y", WIDE),
            P(None, WIDE),
            P(None, WIDE),
            P("y", None, WIDE),
            P("y", None, WIDE),
            P(WIDE),
            P(WIDE),
            P(WIDE),
            P("y", WIDE, None, None),
            P(WIDE),
            P(WIDE, "y"),
        ),
        out_specs=P(None, WIDE, "y"),
        check_vma=False,
    )
```

```python
import functools

import jax
import ml_dtypes
import numpy as np
import jax.numpy as jnp
from jax import lax
from jax.experimental import pallas as pl
from jax.experimental.pallas import tpu as pltpu
from jax.sharding import Mesh
from jax.sharding import PartitionSpec as P

D = 8192
GROUPS = 8
DI = 16384
STEPS = 5
CONVK = 4
EPS = 1e-05

NZ, NX, NC, NY = 8, 4, 2, 8
OWN = 3
SLOT = 16
HALF = NX * SLOT
BLOCK = NC * HALF
RB = 24
BF = jnp.bfloat16
F32 = jnp.float32
WIDE = ("z", "x", "core")


def swap_core(v):
    return lax.ppermute(v, "core", [(0, 1), (1, 0)])


def to_all(v, axes, count):
    return lax.all_to_all(
        jnp.broadcast_to(v[None], (count,) + v.shape), axes, split_axis=0, concat_axis=0, tiled=True
    )


NEXT, ACROSS, PREVIOUS = ([(i, (i + k) % NX) for i in range(NX)] for k in (1, 2, 3))


def around_x(v):
    return [v] + [lax.ppermute(v, "x", way) for way in (NEXT, ACROSS, PREVIOUS)]


def exchange(v, axes):
    return lax.all_to_all(v, axes, split_axis=0, concat_axis=0, tiled=True)


def call(kernel, out_shape, in_specs, vmem=32, **kw):
    return pl.pallas_call(
        kernel,
        out_shape=out_shape,
        in_specs=in_specs,
        compiler_params=pltpu.CompilerParams(vmem_limit_bytes=vmem * 2**20),
        **kw,
    )


VM = pl.BlockSpec(memory_space=pltpu.VMEM)
SM = pl.BlockSpec(memory_space=pltpu.SMEM)


def over(lhs, w, k):
    return lax.dot_general(lhs, w, (((1,), (k,)), ((), ())), preferred_element_type=F32)


def into_empty(values, lanes, rows):
    slot = lax.broadcasted_iota(jnp.int32, rows.shape, 0) % SLOT
    total = jnp.sum(values.reshape(-1, SLOT, 128), axis=1, keepdims=True)
    total = jnp.broadcast_to(total, (rows.shape[0] // SLOT, SLOT, 128)).reshape(rows.shape)
    return jnp.where((slot == SLOT - 1) & lanes, total, rows)


def small_kernel(pos_ref, g_ref, gain_ref, w_ref, w_other_ref, out_ref):
    raw = g_ref[...].reshape(NX * NZ * SLOT, -1).astype(F32)
    lhs = (raw * gain_ref[...]).astype(BF)
    out = over(lhs, jnp.concatenate([w_ref[:64], w_other_ref[:64]], axis=0), 1)
    ss = jnp.sum(raw * raw, axis=1, keepdims=True)
    hi = ss.astype(BF).astype(F32)
    lane = lax.broadcasted_iota(jnp.int32, out.shape, 1) % 64
    slot = lax.broadcasted_iota(jnp.int32, out.shape, 0) % SLOT
    ss = jnp.where(lane == slot, hi, jnp.where(lane == slot + SLOT, ss - hi, 0.0))
    out = into_empty(ss, lane < 2 * SLOT, out).reshape(NX, NZ, SLOT, 128)
    for x in range(2):
        low, high = out[x], out[x + 2]
        rows = slice(x * SLOT, x * SLOT + SLOT)
        own = jnp.concatenate([low[:, :, :64], high[:, :, :64]], axis=2)
        other = jnp.concatenate([low[:, :, 64:], high[:, :, 64:]], axis=2)
        out_ref[pos_ref[0], :, rows] = own.astype(BF)
        out_ref[1 - pos_ref[0], :, rows] = other.astype(BF)


def large_kernel(pos_ref, g_ref, gain_ref, *refs):
    weights, out_ref = refs[:6], refs[6]
    size = NZ * SLOT
    lhs = (g_ref[...].reshape(NX * size, -1).astype(F32) * gain_ref[...]).astype(BF)
    heads = [
        jnp.broadcast_to(ref[h : h + 1, :].astype(F32), (SLOT, D // NY))
        for ref in weights[4:]
        for h in range(64, 68)
    ]
    sizes = over(lhs, jnp.concatenate(heads, axis=0).astype(BF), 1)
    lane = lax.broadcasted_iota(jnp.int32, sizes.shape, 1)
    slot = lax.broadcasted_iota(jnp.int32, sizes.shape, 0) % SLOT
    sizes = jnp.where(lane % SLOT == slot, sizes, 0.0)
    sizes = (sizes, pltpu.roll(sizes, 64, 1))
    core = pos_ref[0]
    for i, w_ref in enumerate(weights[:4]):
        to, cols = (core, 1 - core)[i // 2], slice(i % 2 * 256, i % 2 * 256 + 256)
        out = jnp.dot(lhs, w_ref[...], preferred_element_type=F32)
        if i % 2 == 0:
            first = into_empty(sizes[i // 2], lane < 64, out[:, :128])
            out = jnp.concatenate([first, out[:, 128:]], axis=1)
        out = out.astype(BF)
        for x in range(NX):
            out_ref[to, :, x * SLOT : x * SLOT + SLOT, cols] = out[
                x * size : x * size + size
            ].reshape(NZ, SLOT, 256)


def slot_of(m):
    core, x, j = m // HALF, m % HALF // SLOT, m % SLOT
    step = (j * 11) // 32
    q = x * NC + core
    return step * RB + q * OWN + (j - step * OWN), j, q


def step_from_slot():
    i = lax.broadcasted_iota(jnp.int32, (STEPS * RB, BLOCK), 0)
    at, j, _ = slot_of(lax.broadcasted_iota(jnp.int32, (STEPS * RB, BLOCK), 1))
    return jnp.where((at == i) & (j < SLOT - 1), 1.0, 0.0).astype(BF)


def slot_from_step():
    shape = (BLOCK, STEPS * RB)
    at, j, q = slot_of(lax.broadcasted_iota(jnp.int32, shape, 0))
    i = lax.broadcasted_iota(jnp.int32, shape, 1)
    row = i % RB
    last = j == SLOT - 1
    order = jnp.where((at == i) & ~last, 1.0, 0.0).astype(BF)
    collect = jnp.where((row // OWN == q) & last, 1.0, 0.0).astype(BF)
    return order, collect


def conv(hist_ref, current, taps):
    seq = [hist_ref[k].astype(F32) for k in range(CONVK - 1)]
    seq += [current[t * RB : (t + 1) * RB] for t in range(STEPS)]
    out = []
    for t in range(STEPS):
        acc = taps[0:1] * seq[t]
        for k in range(1, CONVK):
            acc = acc + taps[k : k + 1] * seq[t + k]
        out.append(acc * jax.nn.sigmoid(acc))
    return out


def empty_sums(rows):
    slot = lax.broadcasted_iota(jnp.int32, rows.shape, 0) % SLOT
    lane = lax.broadcasted_iota(jnp.int32, rows.shape, 1)
    mask = (lane == slot) | (lane == slot + SLOT)
    shape = (rows.shape[0] // SLOT, SLOT, rows.shape[1])
    ss = jnp.broadcast_to(rows.reshape(shape)[:, SLOT - 1 :], shape).reshape(rows.shape)
    return jnp.sum(jnp.where(mask, ss, 0.0), axis=1, keepdims=True)


def shared_kernel(p_ref, hist_ref, taps_ref, rstd_ref, bcc_ref):
    total = []
    for c in range(NC):
        part = p_ref[c * NY].astype(F32)
        for n in range(1, NY):
            part = part + p_ref[c * NY + n].astype(F32)
        total += [part[:, :64], part[:, 64:]]
    total = jnp.concatenate(total, axis=0)
    rest = rstd = lax.rsqrt(empty_sums(total) / D + EPS)
    lane = lax.broadcasted_iota(jnp.int32, total.shape, 1)
    factor = jnp.zeros(total.shape, F32)
    for k in range(3):
        piece = rest.astype(BF).astype(F32)
        factor = jnp.where(lane == k, piece, factor)
        rest = rest - piece
    raw = jnp.concatenate([total * rstd, factor], axis=1).astype(BF)
    cur = jnp.dot(step_from_slot(), raw, preferred_element_type=F32)
    rstd = cur[:, 64:65] + cur[:, 65:66] + cur[:, 66:67]
    rstd_ref[...] = jnp.broadcast_to(rstd, rstd_ref.shape)
    out = conv(hist_ref, cur[:, :64], taps_ref[...]) + [jnp.zeros((8, 64), F32)]
    out = jnp.concatenate(out, axis=0)
    bcc_ref[...] = jnp.concatenate([out[:64], out[64:]], axis=1).astype(BF)


def at(v, t):
    return v[t * RB : (t + 1) * RB]


def carried_kernel(
    pos_ref, bc_0, bc_1, bc_2, bc_3, rstd_ref, s_ref, out_ref, c_rows, y_rows, held
):
    core, here = pos_ref[0], pos_ref[1]
    for k, ref in enumerate((bc_0, bc_1, bc_2, bc_3)):
        frm = (here + NX - k) % NX
        held[frm * NC + core] = ref[0].astype(F32)
        held[frm * NC + 1 - core] = ref[1].astype(F32)
    vectors = [held[i] for i in range(NX * NC)]
    vectors = [jnp.concatenate([v[:, :64], v[:, 64:]], axis=0) for v in vectors]
    b_vec = jnp.concatenate(vectors[:4], axis=1)
    c_vec = jnp.concatenate(vectors[4:], axis=1)

    c_rows[...] = jnp.zeros_like(c_rows)
    for t in range(STEPS):
        for h in range(2):
            c_rows[h, pl.ds(t, RB, stride=8), :] = at(c_vec, t)[:, h * 128 : h * 128 + 128]
    for r in range(RB):
        c_row = jnp.concatenate([c_rows[h, r * 8 : r * 8 + 8, :] for h in range(2)], axis=1)
        y_row = lax.dot_general(
            c_row.astype(BF), s_ref[r], (((1,), (1,)), ((), ())), preferred_element_type=F32
        )
        for h in range(2):
            y_rows[h, r * 8 : r * 8 + 8, :] = y_row[:, h * 128 : h * 128 + 128]

    for t in range(STEPS):
        for h in range(2):
            out_ref[t * RB : t * RB + RB, h * 128 : h * 128 + 128] = y_rows[h, pl.ds(t, RB, stride=8), :]
    rstd = rstd_ref[...]
    lane = lax.broadcasted_iota(jnp.int32, (RB, 128), 1)
    for t in range(STEPS):
        out = at(rstd, t)
        for s in range(t + 1):
            pair = jnp.sum(at(c_vec, t) * at(b_vec, s), axis=1, keepdims=True)
            out = jnp.where(lane == s, pair, out)
        out_ref[t * RB : t * RB + RB, 256:] = out


def orders():
    m = np.arange(NC * NY * HALF)[None]
    i = np.arange(STEPS * RB)[:, None]
    x, j = m % HALF // SLOT, m % SLOT
    q = x * NC + m // (NY * HALF)
    row = np.where(j < SLOT - 1, j // OWN * RB + q * OWN + j % OWN, -1)
    empty = (q == i % RB // OWN) & (j == SLOT - 1)
    return jnp.asarray(np.concatenate([row == i, empty]).astype(ml_dtypes.bfloat16))


def state_kernel(ready_ref, p_ref, params_ref, hist_ref, orders_ref, u_ref):
    taps, gain = params_ref[0:4], params_ref[4:5]
    a_log, bias, skip = params_ref[5:6], params_ref[6:7], params_ref[7:8]
    y0, pairs = ready_ref[:, :256], ready_ref[:, 256:]
    rstd = pairs[:, 127:]
    large = p_ref[...].reshape(NC * NY * HALF, 512)
    sizes = jnp.dot(orders_ref[STEPS * RB :], large[:, :128], preferred_element_type=F32) * rstd
    row = lax.broadcasted_iota(jnp.int32, sizes.shape, 0)
    lane = lax.broadcasted_iota(jnp.int32, sizes.shape, 1)
    slot = row // RB * OWN + row % RB % OWN
    sizes = jnp.where((lane % SLOT == slot) & (lane < 64), sizes, 0.0).astype(BF)
    lane = lax.broadcasted_iota(jnp.int32, (128, 256), 0)
    head = lax.broadcasted_iota(jnp.int32, (128, 256), 1) // 64
    spread = jnp.where(lane // SLOT == head, 1.0, 0.0).astype(BF)
    pre = jnp.dot(sizes, spread, preferred_element_type=F32) + bias
    dt = jnp.maximum(pre, 0.0) + jnp.log1p(jnp.exp(-jnp.abs(pre)))
    decay = jnp.exp(-dt * jnp.exp(a_log))
    order, collect = slot_from_step()
    raw = jnp.dot(orders_ref[: STEPS * RB], large, preferred_element_type=F32) * rstd
    raw = raw.astype(BF).astype(F32)
    gate = raw[:, 256:]
    gate = gate * jax.nn.sigmoid(gate)
    inner = conv(hist_ref, raw[:, :256], taps)
    carried, terms, gated = None, [], []
    for t in range(STEPS):
        d = at(decay, t)
        carried = d if carried is None else carried * d
        terms = [term * d for term in terms] + [at(dt, t) * inner[t]]
        y = carried * at(y0, t) + skip * inner[t]
        for s in range(t + 1):
            y = y + at(pairs, t)[:, s : s + 1] * terms[s]
        gated.append(y * at(gate, t))
    gated = jnp.concatenate(gated, axis=0)
    ss = jnp.sum(gated * gated, axis=1, keepdims=True)
    hi = ss.astype(BF).astype(F32)
    lo = ss - hi
    row = lax.broadcasted_iota(jnp.int32, gated.shape, 0)
    lane = lax.broadcasted_iota(jnp.int32, gated.shape, 1)
    slot = row // RB * OWN + row % RB % OWN
    sums = jnp.where(lane == slot, hi, jnp.where(lane == slot + SLOT, lo, 0.0)).astype(BF)
    u = jnp.dot(order, (gated * gain).astype(BF), preferred_element_type=F32)
    u = (u + jnp.dot(collect, sums, preferred_element_type=F32)).astype(BF)
    for x in range(NX):
        for c in range(NC):
            first = c * HALF + x * SLOT
            for n in range(NY):
                u_ref[x, n, c] = u[first : first + SLOT]


def out_kernel(own, pos_ref, u_ref, w_ref, left_ref, low_ref, high_ref, right_ref, o_ref):
    core, here = pos_ref[0], pos_ref[1]
    which = core if own else 1 - core
    rows = [
        u_ref[(here + NX - k) % NX, :, which].reshape(NY * SLOT, 256) for k in range(NX)
    ]
    ss = rows[0][:, :128].astype(F32)
    for r in rows[1:]:
        ss = ss + r[:, :128].astype(F32)
    if not own:
        lane = lax.broadcasted_iota(jnp.int32, ss.shape, 1)
        ss = ss + pltpu.roll(ss, 128 - SLOT, 1)
        hi = ss.astype(BF).astype(F32)
        lo = pltpu.roll(ss - hi, SLOT, 1)
        ss = jnp.where(lane < SLOT, hi, jnp.where(lane < 2 * SLOT, lo, 0.0))
    dot = lambda v, w: jnp.dot(v, w[...], preferred_element_type=F32)
    total = dot(rows[0], w_ref) + dot(rows[1], left_ref) + dot(rows[3], right_ref)
    total = total + dot(rows[2][:, :128], low_ref) + dot(rows[2][:, 128:], high_ref)
    slot = lax.broadcasted_iota(jnp.int32, ss.shape, 0) % SLOT
    first = jnp.where(slot == SLOT - 1, ss, total[:, :128])
    total = jnp.concatenate([first, total[:, 128:]], axis=1)
    o_ref[...] = total.astype(o_ref.dtype).reshape(o_ref.shape)


def group_kernel(own_ref, other_ref, o_ref):
    total = own_ref[...] + other_ref[...].reshape(NZ * SLOT, -1).astype(F32)
    total = total * lax.rsqrt(empty_sums(total[:, :128]) / (DI // GROUPS) + EPS)
    o_ref[...] = total.astype(BF).reshape(o_ref.shape)


def last_kernel(p_ref, x_ref, o_ref):
    acc = x_ref[...].astype(F32)
    for z in range(NZ):
        acc = acc + p_ref[z].astype(F32)
    for t in range(STEPS):
        o_ref[t] = acc[t * OWN : t * OWN + OWN].astype(BF)


def per_device(
    inputs, pre_gain, w_z, w_x, w_bc, w_dt, conv_x_w, conv_bc_w, conv_x_state, conv_bc_state,
    a_log, dt_bias, skip_d, ssm_state, norm_gain, w_out,
):
    shape = jax.ShapeDtypeStruct
    pos = jnp.stack([lax.axis_index("core"), lax.axis_index("x")]).astype(jnp.int32)
    tokens = jnp.pad(inputs.reshape(STEPS * OWN, -1), ((0, 1), (0, 0)))
    gathered = to_all(to_all(tokens, "z", NZ), "x", NX)
    gain = pre_gain[None]
    w_small = jnp.concatenate([w_bc.T, w_dt.T, jnp.zeros((12, w_bc.shape[0]), BF)], axis=0)
    w_small_other = swap_core(w_small)
    small = call(small_kernel, shape((NC, NY, HALF // 2, 128), BF), [SM] + [VM] * 4)(
        pos, gathered, gain, w_small, w_small_other
    )
    weights = (w_x, w_z, swap_core(w_x), swap_core(w_z), w_small, w_small_other)
    large = call(large_kernel, shape((NC, NY, HALF, 512), BF), [SM] + [VM] * 8)(
        pos, gathered, gain, *weights
    )
    small, a_log, dt_bias, skip_d, norm_gain, conv_x_w = lax.optimization_barrier(
        (small, a_log, dt_bias, skip_d, norm_gain, conv_x_w)
    )
    heads = jnp.repeat(jnp.stack([a_log, dt_bias, skip_d]), 64, axis=1)
    params = jnp.concatenate([conv_x_w, norm_gain[None], heads], axis=0)

    small = exchange(small.reshape(NC * NY, HALF // 2, 128), ("core", "y"))
    rstd, bcc = call(
        shared_kernel, (shape((STEPS * RB, 128), F32), shape((64, 128), BF)), [VM] * 3
    )(small, jnp.swapaxes(conv_bc_state, 0, 1), conv_bc_w)
    large, bcc, w_out = lax.optimization_barrier((large, bcc, w_out))
    left, right = (lax.ppermute(w_out, "x", way) for way in (NEXT, PREVIOUS))
    large = exchange(large.reshape(NC * NY, HALF, 512), ("core", "y"))
    ready = call(
        carried_kernel,
        shape((STEPS * RB, 384), F32),
        [SM] + [VM] * 6,
        scratch_shapes=[pltpu.VMEM((2, RB * 8, 128), F32)] * 2
        + [pltpu.VMEM((NX * NC, 64, 128), F32)],
    )(
        pos, *around_x(jnp.stack([bcc, swap_core(bcc)])), rstd, ssm_state.reshape(RB, 256, 256)
    )
    ready, left, right = lax.optimization_barrier((ready, left, right))
    u = call(state_kernel, shape((NX, NY, NC, SLOT, 256), BF), [VM] * 5)(
        ready, large, params, jnp.swapaxes(conv_x_state, 0, 1), orders()
    )
    u = exchange(u.reshape(NX * NY, NC, SLOT, 256), ("x", "y")).reshape(u.shape)
    half = w_out.shape[0] // 2
    low = lax.ppermute(left[:half], "x", NEXT)
    high = lax.ppermute(right[half:], "x", PREVIOUS)
    width = w_out.shape[1]
    out = lambda own, result: call(
        functools.partial(out_kernel, own), result, [SM] + [VM] * 6
    )(pos, u, w_out, left, low, high, right)
    other = swap_core(out(False, shape((NZ, SLOT, width), BF)))
    sums = call(group_kernel, shape((NZ, SLOT, width), BF), [VM] * 2)(
        out(True, shape((NZ * SLOT, width), F32)), other
    )
    return call(last_kernel, shape(inputs.shape, BF), [VM] * 2)(exchange(sums, "z"), tokens)


def solution(mesh):
    fine = Mesh(mesh.devices.reshape(NZ, NX, NC, NY), (*WIDE, "y"))
    return jax.shard_map(
        per_device,
        mesh=fine,
        in_specs=(
            P(None, WIDE, "y"),
            P("y"),
            P("y", WIDE),
            P("y", WIDE),
            P("y", WIDE),
            P("y", WIDE),
            P(None, WIDE),
            P(None, WIDE),
            P("y", None, WIDE),
            P("y", None, WIDE),
            P(WIDE),
            P(WIDE),
            P(WIDE),
            P("y", WIDE, None, None),
            P(WIDE),
            P(WIDE, "y"),
        ),
        out_specs=P(None, WIDE, "y"),
        check_vma=False,
    )
```

```python
import functools

import jax
import ml_dtypes
import numpy as np
import jax.numpy as jnp
from jax import lax
from jax.experimental import pallas as pl
from jax.experimental.pallas import tpu as pltpu
from jax.sharding import Mesh
from jax.sharding import PartitionSpec as P

D = 8192
GROUPS = 8
DI = 16384
STEPS = 5
CONVK = 4
EPS = 1e-05

NZ, NX, NC, NY = 8, 4, 2, 8
OWN = 3
SLOT = 16
HALF = NX * SLOT
BLOCK = NC * HALF
RB = 24
BF = jnp.bfloat16
F32 = jnp.float32
WIDE = ("z", "x", "core")


def swap_core(v):
    return lax.ppermute(v, "core", [(0, 1), (1, 0)])


def to_all(v, axes, count):
    return lax.all_to_all(
        jnp.broadcast_to(v[None], (count,) + v.shape), axes, split_axis=0, concat_axis=0, tiled=True
    )


NEXT, ACROSS, PREVIOUS = ([(i, (i + k) % NX) for i in range(NX)] for k in (1, 2, 3))


def around_x(v):
    return [v] + [lax.ppermute(v, "x", way) for way in (NEXT, ACROSS, PREVIOUS)]


def exchange(v, axes):
    return lax.all_to_all(v, axes, split_axis=0, concat_axis=0, tiled=True)


def call(kernel, out_shape, in_specs, vmem=32, **kw):
    return pl.pallas_call(
        kernel,
        out_shape=out_shape,
        in_specs=in_specs,
        compiler_params=pltpu.CompilerParams(vmem_limit_bytes=vmem * 2**20),
        **kw,
    )


VM = pl.BlockSpec(memory_space=pltpu.VMEM)
SM = pl.BlockSpec(memory_space=pltpu.SMEM)


def over(lhs, w, k):
    return lax.dot_general(lhs, w, (((1,), (k,)), ((), ())), preferred_element_type=F32)


def into_empty(values, lanes, rows):
    slot = lax.broadcasted_iota(jnp.int32, rows.shape, 0) % SLOT
    total = jnp.sum(values.reshape(-1, SLOT, 128), axis=1, keepdims=True)
    total = jnp.broadcast_to(total, (rows.shape[0] // SLOT, SLOT, 128)).reshape(rows.shape)
    return jnp.where((slot == SLOT - 1) & lanes, total, rows)


def small_kernel(pos_ref, g_ref, gain_ref, w_ref, w_other_ref, out_ref):
    raw = g_ref[...].reshape(NX * NZ * SLOT, -1).astype(F32)
    lhs = (raw * gain_ref[...]).astype(BF)
    out = over(lhs, jnp.concatenate([w_ref[:64], w_other_ref[:64]], axis=0), 1)
    ss = jnp.sum(raw * raw, axis=1, keepdims=True)
    hi = ss.astype(BF).astype(F32)
    lane = lax.broadcasted_iota(jnp.int32, out.shape, 1) % 64
    slot = lax.broadcasted_iota(jnp.int32, out.shape, 0) % SLOT
    ss = jnp.where(lane == slot, hi, jnp.where(lane == slot + SLOT, ss - hi, 0.0))
    out = into_empty(ss, lane < 2 * SLOT, out).astype(BF).reshape(NX, NZ, SLOT, 128)
    for x in range(2):
        low, high = out[x], out[x + 2]
        rows = slice(x * SLOT, x * SLOT + SLOT)
        own = jnp.concatenate([low[:, :, :64], high[:, :, :64]], axis=2)
        other = jnp.concatenate([low[:, :, 64:], high[:, :, 64:]], axis=2)
        out_ref[pos_ref[0], :, rows] = own
        out_ref[1 - pos_ref[0], :, rows] = other


def large_kernel(pos_ref, g_ref, gain_ref, *refs):
    weights, out_ref = refs[:6], refs[6]
    size = NZ * SLOT
    lhs = (g_ref[...].reshape(NX * size, -1).astype(F32) * gain_ref[...]).astype(BF)
    heads = [
        jnp.broadcast_to(ref[h : h + 1, :].astype(F32), (SLOT, D // NY))
        for ref in weights[4:]
        for h in range(64, 68)
    ]
    sizes = over(lhs, jnp.concatenate(heads, axis=0).astype(BF), 1)
    lane = lax.broadcasted_iota(jnp.int32, sizes.shape, 1)
    slot = lax.broadcasted_iota(jnp.int32, sizes.shape, 0) % SLOT
    sizes = jnp.where(lane % SLOT == slot, sizes, 0.0)
    sizes = (sizes, pltpu.roll(sizes, 64, 1))
    core = pos_ref[0]
    for i, w_ref in enumerate(weights[:4]):
        to, cols = (core, 1 - core)[i // 2], slice(i % 2 * 256, i % 2 * 256 + 256)
        out = jnp.dot(lhs, w_ref[...], preferred_element_type=F32)
        if i % 2 == 0:
            first = into_empty(sizes[i // 2], lane < 64, out[:, :128])
            out = jnp.concatenate([first, out[:, 128:]], axis=1)
        out = out.astype(BF)
        for x in range(NX):
            out_ref[to, :, x * SLOT : x * SLOT + SLOT, cols] = out[
                x * size : x * size + size
            ].reshape(NZ, SLOT, 256)


def slot_of(m):
    core, x, j = m // HALF, m % HALF // SLOT, m % SLOT
    step = (j * 11) // 32
    q = x * NC + core
    return step * RB + q * OWN + (j - step * OWN), j, q


def step_from_slot():
    i = lax.broadcasted_iota(jnp.int32, (STEPS * RB, BLOCK), 0)
    at, j, _ = slot_of(lax.broadcasted_iota(jnp.int32, (STEPS * RB, BLOCK), 1))
    return jnp.where((at == i) & (j < SLOT - 1), 1.0, 0.0).astype(BF)


def slot_from_step():
    shape = (BLOCK, STEPS * RB)
    at, j, q = slot_of(lax.broadcasted_iota(jnp.int32, shape, 0))
    i = lax.broadcasted_iota(jnp.int32, shape, 1)
    row = i % RB
    last = j == SLOT - 1
    order = jnp.where((at == i) & ~last, 1.0, 0.0).astype(BF)
    collect = jnp.where((row // OWN == q) & last, 1.0, 0.0).astype(BF)
    return order, collect


def conv(hist_ref, current, taps):
    seq = [hist_ref[k].astype(F32) for k in range(CONVK - 1)]
    seq += [current[t * RB : (t + 1) * RB] for t in range(STEPS)]
    out = []
    for t in range(STEPS):
        acc = taps[0:1] * seq[t]
        for k in range(1, CONVK):
            acc = acc + taps[k : k + 1] * seq[t + k]
        out.append(acc * jax.nn.sigmoid(acc))
    return out


def empty_sums(rows):
    slot = lax.broadcasted_iota(jnp.int32, rows.shape, 0) % SLOT
    lane = lax.broadcasted_iota(jnp.int32, rows.shape, 1)
    mask = (lane == slot) | (lane == slot + SLOT)
    shape = (rows.shape[0] // SLOT, SLOT, rows.shape[1])
    ss = jnp.broadcast_to(rows.reshape(shape)[:, SLOT - 1 :], shape).reshape(rows.shape)
    return jnp.sum(jnp.where(mask, ss, 0.0), axis=1, keepdims=True)


def shared_kernel(p_ref, hist_ref, taps_ref, rstd_ref, bcc_ref):
    total = []
    for c in range(NC):
        part = p_ref[c * NY].astype(F32)
        for n in range(1, NY):
            part = part + p_ref[c * NY + n].astype(F32)
        total += [part[:, :64], part[:, 64:]]
    total = jnp.concatenate(total, axis=0)
    rest = rstd = lax.rsqrt(empty_sums(total) / D + EPS)
    lane = lax.broadcasted_iota(jnp.int32, total.shape, 1)
    factor = jnp.zeros(total.shape, F32)
    for k in range(3):
        piece = rest.astype(BF).astype(F32)
        factor = jnp.where(lane == k, piece, factor)
        rest = rest - piece
    raw = jnp.concatenate([total * rstd, factor], axis=1).astype(BF)
    cur = jnp.dot(step_from_slot(), raw, preferred_element_type=F32)
    rstd = cur[:, 64:65] + cur[:, 65:66] + cur[:, 66:67]
    rstd_ref[...] = jnp.broadcast_to(rstd, rstd_ref.shape)
    out = conv(hist_ref, cur[:, :64], taps_ref[...]) + [jnp.zeros((8, 64), F32)]
    out = jnp.concatenate(out, axis=0)
    bcc_ref[...] = jnp.concatenate([out[:64], out[64:]], axis=1).astype(BF)


def at(v, t):
    return v[t * RB : (t + 1) * RB]


def carried_kernel(
    pos_ref, bc_0, bc_1, bc_2, bc_3, rstd_ref, s_ref, out_ref, c_rows, y_rows, held
):
    core, here = pos_ref[0], pos_ref[1]
    for k, ref in enumerate((bc_0, bc_1, bc_2, bc_3)):
        frm = (here + NX - k) % NX
        held[frm * NC + core] = ref[0].astype(F32)
        held[frm * NC + 1 - core] = ref[1].astype(F32)
    vectors = [held[i] for i in range(NX * NC)]
    vectors = [jnp.concatenate([v[:, :64], v[:, 64:]], axis=0) for v in vectors]
    b_vec = jnp.concatenate(vectors[:4], axis=1)
    c_vec = jnp.concatenate(vectors[4:], axis=1)

    c_rows[...] = jnp.zeros_like(c_rows)
    for t in range(STEPS):
        for h in range(2):
            c_rows[h, pl.ds(t, RB, stride=8), :] = at(c_vec, t)[:, h * 128 : h * 128 + 128]
    for r in range(RB):
        c_row = jnp.concatenate([c_rows[h, r * 8 : r * 8 + 8, :] for h in range(2)], axis=1)
        y_row = lax.dot_general(
            c_row.astype(BF), s_ref[r], (((1,), (1,)), ((), ())), preferred_element_type=F32
        )
        for h in range(2):
            y_rows[h, r * 8 : r * 8 + 8, :] = y_row[:, h * 128 : h * 128 + 128]

    for t in range(STEPS):
        for h in range(2):
            out_ref[t * RB : t * RB + RB, h * 128 : h * 128 + 128] = y_rows[h, pl.ds(t, RB, stride=8), :]
    rstd = rstd_ref[...]
    lane = lax.broadcasted_iota(jnp.int32, (RB, 128), 1)
    for t in range(STEPS):
        out = at(rstd, t)
        for s in range(t + 1):
            pair = jnp.sum(at(c_vec, t) * at(b_vec, s), axis=1, keepdims=True)
            out = jnp.where(lane == s, pair, out)
        out_ref[t * RB : t * RB + RB, 256:] = out


def orders():
    m = np.arange(NC * NY * HALF)[None]
    i = np.arange(STEPS * RB)[:, None]
    x, j = m % HALF // SLOT, m % SLOT
    q = x * NC + m // (NY * HALF)
    row = np.where(j < SLOT - 1, j // OWN * RB + q * OWN + j % OWN, -1)
    empty = (q == i % RB // OWN) & (j == SLOT - 1)
    return jnp.asarray(np.concatenate([row == i, empty]).astype(ml_dtypes.bfloat16))


def state_kernel(ready_ref, p_ref, params_ref, hist_ref, orders_ref, u_ref):
    taps, gain = params_ref[0:4], params_ref[4:5]
    a_log, bias, skip = params_ref[5:6], params_ref[6:7], params_ref[7:8]
    y0, pairs = ready_ref[:, :256], ready_ref[:, 256:]
    rstd = pairs[:, 127:]
    large = p_ref[...].reshape(NC * NY * HALF, 512)
    sizes = jnp.dot(orders_ref[STEPS * RB :], large[:, :128], preferred_element_type=F32) * rstd
    row = lax.broadcasted_iota(jnp.int32, sizes.shape, 0)
    lane = lax.broadcasted_iota(jnp.int32, sizes.shape, 1)
    slot = row // RB * OWN + row % RB % OWN
    sizes = jnp.where((lane % SLOT == slot) & (lane < 64), sizes, 0.0).astype(BF)
    lane = lax.broadcasted_iota(jnp.int32, (128, 256), 0)
    head = lax.broadcasted_iota(jnp.int32, (128, 256), 1) // 64
    spread = jnp.where(lane // SLOT == head, 1.0, 0.0).astype(BF)
    pre = jnp.dot(sizes, spread, preferred_element_type=F32) + bias
    dt = jnp.maximum(pre, 0.0) + jnp.log1p(jnp.exp(-jnp.abs(pre)))
    decay = jnp.exp(-dt * jnp.exp(a_log))
    order, collect = slot_from_step()
    raw = jnp.dot(orders_ref[: STEPS * RB], large, preferred_element_type=F32) * rstd
    raw = raw.astype(BF).astype(F32)
    gate = raw[:, 256:]
    gate = gate * jax.nn.sigmoid(gate)
    inner = conv(hist_ref, raw[:, :256], taps)
    carried, terms, gated = None, [], []
    for t in range(STEPS):
        d = at(decay, t)
        carried = d if carried is None else carried * d
        terms = [term * d for term in terms] + [at(dt, t) * inner[t]]
        y = carried * at(y0, t) + skip * inner[t]
        for s in range(t + 1):
            y = y + at(pairs, t)[:, s : s + 1] * terms[s]
        gated.append(y * at(gate, t))
    gated = jnp.concatenate(gated, axis=0)
    ss = jnp.sum(gated * gated, axis=1, keepdims=True)
    hi = ss.astype(BF).astype(F32)
    lo = ss - hi
    row = lax.broadcasted_iota(jnp.int32, gated.shape, 0)
    lane = lax.broadcasted_iota(jnp.int32, gated.shape, 1)
    slot = row // RB * OWN + row % RB % OWN
    sums = jnp.where(lane == slot, hi, jnp.where(lane == slot + SLOT, lo, 0.0)).astype(BF)
    u = jnp.dot(order, (gated * gain).astype(BF), preferred_element_type=F32)
    u = (u + jnp.dot(collect, sums, preferred_element_type=F32)).astype(BF)
    for x in range(NX):
        for c in range(NC):
            first = c * HALF + x * SLOT
            for n in range(NY):
                u_ref[x, n, c] = u[first : first + SLOT]


def out_kernel(own, pos_ref, u_ref, w_ref, left_ref, low_ref, high_ref, right_ref, o_ref):
    core, here = pos_ref[0], pos_ref[1]
    which = core if own else 1 - core
    rows = [
        u_ref[(here + NX - k) % NX, :, which].reshape(NY * SLOT, 256) for k in range(NX)
    ]
    ss = rows[0][:, :128].astype(F32)
    for r in rows[1:]:
        ss = ss + r[:, :128].astype(F32)
    if not own:
        lane = lax.broadcasted_iota(jnp.int32, ss.shape, 1)
        ss = ss + pltpu.roll(ss, 128 - SLOT, 1)
        hi = ss.astype(BF).astype(F32)
        lo = pltpu.roll(ss - hi, SLOT, 1)
        ss = jnp.where(lane < SLOT, hi, jnp.where(lane < 2 * SLOT, lo, 0.0))
    dot = lambda v, w: jnp.dot(v, w[...], preferred_element_type=F32)
    total = dot(rows[0], w_ref) + dot(rows[1], left_ref) + dot(rows[3], right_ref)
    total = total + dot(rows[2][:, :128], low_ref) + dot(rows[2][:, 128:], high_ref)
    slot = lax.broadcasted_iota(jnp.int32, ss.shape, 0) % SLOT
    first = jnp.where(slot == SLOT - 1, ss, total[:, :128])
    total = jnp.concatenate([first, total[:, 128:]], axis=1)
    o_ref[...] = total.astype(o_ref.dtype).reshape(o_ref.shape)


def group_kernel(own_ref, other_ref, o_ref):
    total = own_ref[...] + other_ref[...].reshape(NZ * SLOT, -1).astype(F32)
    total = total * lax.rsqrt(empty_sums(total[:, :128]) / (DI // GROUPS) + EPS)
    o_ref[...] = total.astype(BF).reshape(o_ref.shape)


def last_kernel(p_ref, x_ref, o_ref):
    acc = x_ref[...].astype(F32)
    for z in range(NZ):
        acc = acc + p_ref[z].astype(F32)
    for t in range(STEPS):
        o_ref[t] = acc[t * OWN : t * OWN + OWN].astype(BF)


def per_device(
    inputs, pre_gain, w_z, w_x, w_bc, w_dt, conv_x_w, conv_bc_w, conv_x_state, conv_bc_state,
    a_log, dt_bias, skip_d, ssm_state, norm_gain, w_out,
):
    shape = jax.ShapeDtypeStruct
    pos = jnp.stack([lax.axis_index("core"), lax.axis_index("x")]).astype(jnp.int32)
    tokens = jnp.pad(inputs.reshape(STEPS * OWN, -1), ((0, 1), (0, 0)))
    column = to_all(tokens, "z", NZ).reshape(NZ * SLOT, -1)
    gathered = to_all(column, "x", NX)
    gain = pre_gain[None]
    w_small = jnp.concatenate([w_bc.T, w_dt.T, jnp.zeros((12, w_bc.shape[0]), BF)], axis=0)
    w_small_other = swap_core(w_small)
    small = call(small_kernel, shape((NC, NY, HALF // 2, 128), BF), [SM] + [VM] * 4)(
        pos, gathered, gain, w_small, w_small_other
    )
    weights = (w_x, w_z, swap_core(w_x), swap_core(w_z), w_small, w_small_other)
    large = call(large_kernel, shape((NC, NY, HALF, 512), BF), [SM] + [VM] * 8)(
        pos, gathered, gain, *weights
    )
    small, a_log, dt_bias, skip_d, norm_gain, conv_x_w = lax.optimization_barrier(
        (small, a_log, dt_bias, skip_d, norm_gain, conv_x_w)
    )
    heads = jnp.repeat(jnp.stack([a_log, dt_bias, skip_d]), 64, axis=1)
    params = jnp.concatenate([conv_x_w, norm_gain[None], heads], axis=0)

    small = exchange(small.reshape(NC * NY, HALF // 2, 128), ("core", "y"))
    rstd, bcc = call(
        shared_kernel, (shape((STEPS * RB, 128), F32), shape((64, 128), BF)), [VM] * 3
    )(small, jnp.swapaxes(conv_bc_state, 0, 1), conv_bc_w)
    large, bcc, w_out = lax.optimization_barrier((large, bcc, w_out))
    left, right = (lax.ppermute(w_out, "x", way) for way in (NEXT, PREVIOUS))
    large = exchange(large.reshape(NC * NY, HALF, 512), ("core", "y"))
    ready = call(
        carried_kernel,
        shape((STEPS * RB, 384), F32),
        [SM] + [VM] * 6,
        scratch_shapes=[pltpu.VMEM((2, RB * 8 + 8, 128), F32)] * 2
        + [pltpu.VMEM((NX * NC, 64, 128), F32)],
    )(
        pos, *around_x(jnp.stack([bcc, swap_core(bcc)])), rstd, ssm_state.reshape(RB, 256, 256)
    )
    ready, left, right = lax.optimization_barrier((ready, left, right))
    u = call(state_kernel, shape((NX, NY, NC, SLOT, 256), BF), [VM] * 5)(
        ready, large, params, jnp.swapaxes(conv_x_state, 0, 1), orders()
    )
    u = exchange(u.reshape(NX * NY, NC * SLOT, 256), ("x", "y")).reshape(u.shape)
    half = w_out.shape[0] // 2
    low = lax.ppermute(left[:half], "x", NEXT)
    high = lax.ppermute(right[half:], "x", PREVIOUS)
    width = w_out.shape[1]
    out = lambda own, result: call(
        functools.partial(out_kernel, own), result, [SM] + [VM] * 6
    )(pos, u, w_out, left, low, high, right)
    other = swap_core(out(False, shape((NZ, SLOT, width), BF)))
    sums = call(group_kernel, shape((NZ, SLOT, width), BF), [VM] * 2)(
        out(True, shape((NZ * SLOT, width), F32)), other
    )
    return call(last_kernel, shape(inputs.shape, BF), [VM] * 2)(exchange(sums, "z"), tokens)


def solution(mesh):
    fine = Mesh(mesh.devices.reshape(NZ, NX, NC, NY), (*WIDE, "y"))
    return jax.shard_map(
        per_device,
        mesh=fine,
        in_specs=(
            P(None, WIDE, "y"),
            P("y"),
            P("y", WIDE),
            P("y", WIDE),
            P("y", WIDE),
            P("y", WIDE),
            P(None, WIDE),
            P(None, WIDE),
            P("y", None, WIDE),
            P("y", None, WIDE),
            P(WIDE),
            P(WIDE),
            P(WIDE),
            P("y", WIDE, None, None),
            P(WIDE),
            P(WIDE, "y"),
        ),
        out_specs=P(None, WIDE, "y"),
        check_vma=False,
    )
```
